128 devices in a mesh: row: 8 (over y, core), col: 16 (over x, z).
Axes of the slice: x: 4, y: 4, z: 4, core: 2. Of those that a mesh axis runs over, the one named last changes fastest.
Arguments:
- root_factor: float32 [4096, 4096], P('col')
- mid_factor: float32 [2, 1024, 1024], P(None, 'col')
- low_factor: float32 [4, 512, 512], P(None, 'col')
- mid_rows: float32 [2, 4096, 1024], P(None, 'row', 'col'), may hold values from -0.125 to 0.125
- low_parent_rows: float32 [4, 1024, 512], P(None, 'row', 'col'), may hold values from -0.109375 to 0.109375
- low_root_rows: float32 [4, 4096, 512], P(None, 'row', 'col'), may hold values from -0.109375 to 0.109375
- mid_struct: int32 [2, 10], replicated, may hold values from 0 to 15, all different within a row
- low_struct: int32 [4, 12], replicated, may hold values from 0 to 19, all different within a row
- low_parent: int32 [4], replicated, may hold values from 0 to 1
Outputs:
- root_sigma: float32 [4096, 4096], P('row', 'col')
- mid_diag: float32 [2, 1024, 1024], P(None, 'row', 'col')
- mid_cross: float32 [2, 1024, 4096], P(None, 'row', 'col')
- low_diag: float32 [4, 512, 512], P(None, 'row', 'col')
- low_cross_parent: float32 [4, 512, 1024], P(None, 'row', 'col')
- low_cross_root: float32 [4, 512, 4096], P(None, 'row', 'col')
The draws below stay inside these ranges and needn't reach their ends.
Inputs may be any that keep to these rules, and one draw needn't show every extreme that they name: `mid_struct`: each row lists 10 different root blocks; every root block is listed by some row. `low_struct`: each row lists 12 different ancestor blocks; every block is listed by some row.
All inputs are finite; a program needn't handle non-finite values.
Results may differ from the reference program's by a relative error of at most 0.0001.
Values sent between devices are 32-bit elements; how exact they have to be, the bound alone decides.
A program may use at most 128 MiB of HBM per device.

```python
import math
import jax
import jax.numpy as jnp
from jax import lax

BLOCK = 256
ROOT = 4096
MID = 1024
LOW = 512
MID_LIVE = 10
LOW_LIVE = 12
MID_NODES = 2
LOW_NODES = 4


def factor_draw(key, shape_all, jitter):
    scales = jnp.exp(jax.random.uniform(key, shape_all[:-1], minval=math.log(0.6), maxval=math.log(1.6)))
    identity = jnp.eye(shape_all[-1], dtype=jnp.float32)
    return identity * scales[..., None] + jitter * (0.5 / math.sqrt(shape_all[-1]))


def draw_root_factor(key, part):
    key = jax.random.fold_in(key, 11)
    key_one, key_two = jax.random.split(key)
    shape_all = (ROOT, ROOT)
    jitter = jax.random.normal(key_two, shape_all)
    return factor_draw(key_one, shape_all, jitter)


def draw_mid_factor(key, part):
    key = jax.random.fold_in(key, 12)
    key_one, key_two = jax.random.split(key)
    shape_all = (MID_NODES, MID, MID)
    jitter = jax.random.normal(key_two, shape_all)
    return factor_draw(key_one, shape_all, jitter)


def draw_low_factor(key, part):
    key = jax.random.fold_in(key, 13)
    key_one, key_two = jax.random.split(key)
    shape_all = (LOW_NODES, LOW, LOW)
    jitter = jax.random.normal(key_two, shape_all)
    return factor_draw(key_one, shape_all, jitter)


def touch_ends(result, stream_key, smallest, largest):
    shape = result.shape
    place = [jax.random.randint(jax.random.fold_in(stream_key, axis), (), 0, shape[axis]) for axis in range(len(shape))]
    result = result.at[tuple(place)].set(smallest)
    longest = shape.index(max(shape))
    place[longest] = (place[longest] + 1) % shape[longest]
    return result.at[tuple(place)].set(largest)


def shard_levels(rng, dims, cuts, smallest, high):
    loudness = 1.0
    for axis_at, blocks in cuts:
        draws = jax.random.uniform(jax.random.fold_in(jax.random.fold_in(rng, 6), axis_at), (blocks,), jnp.float32, smallest / len(cuts), high / len(cuts))
        loudness = loudness * jnp.repeat(jnp.exp(draws), dims[axis_at] // blocks).reshape((-1,) + (1,) * (len(dims) - 1 - axis_at))
    return loudness


def choose_distinct(rng, rows, amount, top, lift):
    sequence = jax.random.permutation(jax.random.fold_in(rng, 1), amount)
    boost = sequence
    for power in range(3):
        boost = boost * boost // amount
    boost = boost * lift // amount
    lots = jax.random.randint(jax.random.fold_in(rng, 2), (rows, amount), 0, 4096) + boost
    fixed_rows = jax.random.permutation(jax.random.fold_in(rng, 3), rows)[jnp.arange(amount) % rows]
    lots = jnp.where(jnp.arange(rows)[:, None] == fixed_rows[None, :], 1 << 14, lots)
    merit = lots * amount + jnp.arange(amount)
    return lax.top_k(merit.astype(jnp.int32), top)[1].astype(jnp.int32)


def scatter_about(own_key, dims, scale, reach, pieces=(), kind=jnp.bfloat16):
    result = scale * jax.random.normal(own_key, dims, jnp.float32)
    if pieces:
        result = result * shard_levels(own_key, dims, pieces, -0.22, 0.18)
    return jnp.clip(result, -reach, reach).astype(kind)


def setup_inputs(seed: int = 0) -> dict:
    keys = jax.random.split(jax.random.key(seed), 10)
    root_factor = draw_root_factor(jax.random.fold_in(keys[9], 71), 0)
    mid_factor = draw_mid_factor(jax.random.fold_in(keys[9], 71), 0)
    low_factor = draw_low_factor(jax.random.fold_in(keys[9], 71), 0)
    mid_rows = scatter_about(keys[3], (MID_NODES, ROOT, MID), (MID_LIVE * BLOCK) ** -0.5, 0.125, ((1, 8), (2, 16)), jnp.float32)
    low_parent_rows = scatter_about(keys[4], (LOW_NODES, MID, LOW), (LOW_LIVE * BLOCK) ** -0.5, 0.109375, ((1, 8), (2, 16)), jnp.float32)
    low_root_rows = scatter_about(keys[5], (LOW_NODES, ROOT, LOW), (LOW_LIVE * BLOCK) ** -0.5, 0.109375, ((1, 8), (2, 16)), jnp.float32)
    mid_struct = choose_distinct(keys[6], MID_NODES, ROOT // BLOCK, MID_LIVE, 0)
    low_struct = choose_distinct(keys[7], LOW_NODES, (MID + ROOT) // BLOCK, LOW_LIVE, 0)
    low_parent = touch_ends(jax.random.randint(keys[8], (LOW_NODES,), 0, MID_NODES), jax.random.fold_in(keys[8], 1), 0, MID_NODES - 1).astype(jnp.int32)
    return {"root_factor": root_factor, "mid_factor": mid_factor, "low_factor": low_factor, "mid_rows": mid_rows, "low_parent_rows": low_parent_rows, "low_root_rows": low_root_rows, "mid_struct": mid_struct, "low_struct": low_struct, "low_parent": low_parent}


HIGHEST = lax.Precision.HIGHEST


def block_live(total_rows, structure, block_rows):
    block_ids = jnp.arange(total_rows, dtype=jnp.int32) // block_rows
    return jnp.any(block_ids[:, None] == structure[None, :], axis=1).astype(jnp.float32)


def one_node(factor, live_rows, sigma_block):
    lower_tri = jnp.tril(factor)
    y_matrix = jnp.matmul(live_rows, lower_tri, precision=HIGHEST)
    cross_block = -jnp.matmul(y_matrix.T, sigma_block, precision=HIGHEST)
    diag_block = jnp.matmul(lower_tri.T, lower_tri, precision=HIGHEST) - jnp.matmul(cross_block, y_matrix, precision=HIGHEST)
    side_block = -jnp.matmul(sigma_block, y_matrix, precision=HIGHEST)
    return diag_block, cross_block, side_block


def reference(root_factor, mid_factor, low_factor, mid_rows, low_parent_rows, low_root_rows, mid_struct, low_struct, low_parent):
    root_tri = jnp.tril(root_factor)
    root_sigma = jnp.matmul(root_tri.T, root_tri, precision=HIGHEST)
    mid_diags, mid_crosses, mid_sides = [], [], []
    for member in range(MID_NODES):
        live = block_live(ROOT, mid_struct[member], BLOCK)
        diag_block, cross_block, side_block = one_node(mid_factor[member], mid_rows[member] * live[:, None], root_sigma)
        mid_diags.append(diag_block)
        mid_crosses.append(cross_block)
        mid_sides.append(side_block)
    mid_diag = jnp.stack(mid_diags)
    mid_cross = jnp.stack(mid_crosses)
    mid_side = jnp.stack(mid_sides)
    low_diags, low_parents, low_roots = [], [], []
    for member in range(LOW_NODES):
        parent = low_parent[member]
        upper_half = jnp.concatenate([mid_diag[parent], mid_cross[parent]], axis=1)
        lower_half = jnp.concatenate([mid_side[parent], root_sigma], axis=1)
        sigma_block = jnp.concatenate([upper_half, lower_half], axis=0)
        live = block_live(MID + ROOT, low_struct[member], BLOCK)
        stacked = jnp.concatenate([low_parent_rows[member], low_root_rows[member]], axis=0) * live[:, None]
        diag_block, cross_block, unused = one_node(low_factor[member], stacked, sigma_block)
        low_diags.append(diag_block)
        low_parents.append(cross_block[:, :MID])
        low_roots.append(cross_block[:, MID:])
    return root_sigma, mid_diag, mid_cross, jnp.stack(low_diags), jnp.stack(low_parents), jnp.stack(low_roots)
```

```python
import functools

import jax
import jax.numpy as jnp
from jax import lax
from jax.experimental import pallas as pl
from jax.experimental.pallas import tpu as pltpu
from jax.sharding import PartitionSpec as P

BLOCK = 256
ROOT = 4096
MID = 1024
LOW = 512
MIDS = 2
LOWS = 4
MESH = pl.DeviceIdType.MESH
HIGH = lax.Precision.HIGH
F32 = jnp.float32
VMEM = pltpu.VMEM
ANY = pl.ANY


class Net:
    def __init__(self, send_sem, recv_sem):
        self.row = lax.axis_index("row")
        self.col = lax.axis_index("col")
        self.place = {
            "x": lax.div(self.col, 4),
            "z": lax.rem(self.col, 4),
            "y": lax.div(self.row, 2),
            "core": lax.rem(self.row, 2),
        }
        self.send_sem, self.recv_sem, self.used, self.started = send_sem, recv_sem, 0, []

    def at(self, axis, shift):
        if axis == "core":
            return lax.rem(self.place["core"] + shift, 2)
        return lax.rem(self.place[axis] + shift + 4, 4)

    def device(self, **shifts):
        at = {axis: self.at(axis, shifts.get(axis, 0)) for axis in self.place}
        return (at["y"] * 2 + at["core"], at["x"] * 4 + at["z"])

    def greet(self, axes):
        barrier = pltpu.get_barrier_semaphore()
        count = 0
        for axis in axes:
            for shift in (1,) if axis == "core" else (1, -1):
                pl.semaphore_signal(barrier, inc=1, device_id=self.device(**{axis: shift}), device_id_type=MESH)
                count += 1
        pl.semaphore_wait(barrier, count)

    def send(self, src, dst, axis, shift):
        index = self.used
        self.used += 1
        copy = pltpu.make_async_remote_copy(
            src_ref=src,
            dst_ref=dst,
            send_sem=self.send_sem.at[index],
            recv_sem=self.recv_sem.at[index],
            device_id=self.device(**{axis: shift}),
            device_id_type=MESH,
        )
        copy.start()
        self.started.append(copy)
        return copy

    def finish(self):
        for copy in self.started:
            copy.wait_send()


def mult(value, unit):
    return pl.multiple_of(value, unit)


def params(collective_id):
    return pltpu.CompilerParams(collective_id=collective_id, has_side_effects=True, vmem_limit_bytes=60 * 2**20)


class Gather:
    def __init__(self, net, src, dst, whole, half, first, second, local_sem, share=None):
        self.net, self.dst, self.whole, self.half = net, dst, whole, half
        self.first, self.second, self.share = first, second, share
        self.src, self.local_sem = src, local_sem

    def spot(self, a, b):
        at = {self.first: self.net.at(self.first, a), self.second: self.net.at(self.second, b)}
        return at["x"], at["z"]

    def piece(self, a, b):
        return self.whole(self.dst, *self.spot(a, b))

    def part(self, a, b, h):
        return self.half(self.dst, *self.spot(a, b), h)

    def start(self):
        net, own = self.net, self.piece(0, 0)
        self.local = pltpu.make_async_copy(self.src, own, self.local_sem)
        self.local.start()
        self.p1 = [net.send(self.src, own, self.first, s) for s in (1, -1)]
        self.p2 = {0: [net.send(self.src, own, self.second, s) for s in (1, -1)]}

    def onward(self, a):
        piece = self.piece(a, 0)
        self.p2[a] = [self.net.send(piece, piece, self.second, s) for s in (1, -1)]

    def first_ring(self):
        self.fwd = []
        for index, shift in enumerate((1, -1)):
            self.p1[index].wait_recv()
            part = self.part(-shift, 0, index)
            self.fwd.append(self.net.send(part, part, self.first, shift))
            self.onward(-shift)

    def first_end(self):
        for copy in self.fwd:
            copy.wait_recv()
        self.onward(2)

    def second_ring(self, a):
        copies = []
        for index, shift in enumerate((1, -1)):
            self.p2[a][index].wait_recv()
            part = self.part(a, -shift, index)
            copies.append(self.net.send(part, part, self.second, shift))
        self.p2[a] = copies

    def second_end(self, a):
        for copy in self.p2[a]:
            copy.wait_recv()

    def finish(self):
        self.local.wait()


class Scatter:
    def __init__(self, net, axis, part, near, far):
        self.net, self.axis, self.part, self.near, self.far = net, axis, part, near, far

    def start(self):
        opposite = self.net.at(self.axis, 2)
        self.first = [
            self.net.send(self.part(opposite, h), self.near[h], self.axis, shift) for h, shift in enumerate((1, -1))
        ]

    def middle(self):
        self.second = []
        for h, shift in enumerate((1, -1)):
            place = self.net.at(self.axis, shift)
            other = 1 - h
            plain = self.net.send(self.part(place, other), self.far[h][other], self.axis, shift)
            self.first[h].wait_recv()
            self.near[h][...] += self.part(place, h)[...]
            added = self.net.send(self.near[h], self.far[h][h], self.axis, shift)
            self.second += [plain, added]

    def end(self, out):
        for copy in self.second:
            copy.wait_recv()
        for h in range(2):
            out[h][...] = self.part(self.net.at(self.axis, 0), h)[...] + self.far[0][h][...] + self.far[1][h][...]


class TorusScatter:
    def __init__(self, net, part_xz, part_zx, bufs_xz, bufs_zx):
        self.net, self.bufs = net, (bufs_xz, bufs_zx)
        self.stages = [self.stage(axis, part, bufs[0], bufs[1])
                       for axis, part, bufs in (("x", part_xz, bufs_xz), ("z", part_zx, bufs_zx))]

    def stage(self, axis, part, near, far):
        return Scatter(self.net, axis, part, [near.at[0], near.at[1]], [[far.at[s, h] for h in range(2)] for s in range(2)])

    def start(self):
        for stage in self.stages:
            stage.start()

    def middle(self):
        for stage in self.stages:
            stage.middle()

    def turn(self):
        later = []
        for stage, axis, bufs in zip(self.stages, ("z", "x"), self.bufs):
            sums = bufs[2]
            stage.end([sums.at[0], sums.at[1]])
            part = functools.partial(lambda sums, o, h: sums.at[h, o], sums)
            later.append(self.stage(axis, part, bufs[3], bufs[4]))
            later[-1].start()
        self.stages = later

    second_middle = middle

    def end(self, out_xz, out_zx):
        for stage, out in zip(self.stages, (out_xz, out_zx)):
            stage.end(out)


def torus_bufs(rows, lanes):
    return [
        VMEM((2, 4, rows, lanes), F32),
        VMEM((2, 2, 4, rows, lanes), F32),
        VMEM((2, 4, rows, lanes), F32),
        VMEM((2, rows, lanes), F32),
        VMEM((2, 2, rows, lanes), F32),
    ]


def split(a):
    high = a.astype(jnp.bfloat16)
    return high, (a - high.astype(F32)).astype(jnp.bfloat16)


def dot3(a, b):
    go = functools.partial(jnp.dot, preferred_element_type=F32)
    return go(a[0], b[0]) + (go(a[0], b[1]) + go(a[1], b[0]))


class Ring:
    def __init__(self, net, piece, half):
        self.net, self.piece, self.half = net, piece, half

    def start(self):
        own = self.piece(self.net.at("y", 0))
        self.near = [self.net.send(own, own, "y", s) for s in (1, -1)]
        self.pair = [self.net.send(own, own, "core", 1)]

    def middle(self):
        self.far = []
        for index, shift in enumerate((1, -1)):
            self.near[index].wait_recv()
            place = self.net.at("y", -shift)
            part = self.half(place, index)
            self.far.append(self.net.send(part, part, "y", shift))
            whole = self.piece(place)
            self.pair.append(self.net.send(whole, whole, "core", 1))

    def end(self):
        for copy in self.far:
            copy.wait_recv()
        whole = self.piece(self.net.at("y", 2))
        self.pair.append(self.net.send(whole, whole, "core", 1))

    def finish(self):
        for copy in self.pair:
            copy.wait_recv()


def first_kernel(lr, m, r, p, lm, ll, sigma, m_all, r_all, q_all, lm_all, ll_all, p_all, q_own, terms, *scratch):
    bufs_xz, bufs_zx, (send_sem, recv_sem, local_sem) = scratch[:5], scratch[5:10], scratch[10:]
    net = Net(send_sem, recv_sem)
    net.greet(("x", "z", "y", "core"))
    core, y = net.place["core"], net.place["y"]

    def rows(x, z, n):
        return pl.ds(mult((x * 4 + z) * n, n), n)

    def eighth(n):
        return pl.ds(mult(y * n, n), n)

    two = pl.ds(2 * core, 2)
    ga_p = Gather(
        net, p, p_all,
        lambda ref, x, z: ref.at[:, rows(x, z, 32), :],
        lambda ref, x, z, h: ref.at[pl.ds(2 * h, 2), rows(x, z, 32), :],
        "x", "z", local_sem.at[0],
    )
    ga_ll = Gather(
        net, ll.at[two, eighth(8), :], ll_all,
        lambda ref, x, z: ref.at[two, x * 4 + z, eighth(8), :],
        lambda ref, x, z, h: ref.at[2 * core + h, x * 4 + z, eighth(8), :],
        "z", "x", local_sem.at[1],
    )
    ga_lm = Gather(
        net, lm.at[core, eighth(16), :], lm_all,
        lambda ref, x, z: ref.at[core, x * 4 + z, eighth(16), :],
        lambda ref, x, z, h: ref.at[core, x * 4 + z, pl.ds(mult(y * 16 + 8 * h, 8), 8), :],
        "x", "z", local_sem.at[2],
    )
    ga_m = Gather(
        net, m, m_all,
        lambda ref, x, z: ref.at[:, rows(x, z, 64), :],
        lambda ref, x, z, h: ref.at[h, rows(x, z, 64), :],
        "x", "z", local_sem.at[3],
    )
    ga_r = Gather(
        net, r, r_all,
        lambda ref, x, z: ref.at[:, rows(x, z, 32), :],
        lambda ref, x, z, h: ref.at[pl.ds(2 * h, 2), rows(x, z, 32), :],
        "z", "x", local_sem.at[4],
    )
    small, large = (ga_p, ga_ll, ga_lm), (ga_m, ga_r)
    ring_ll = Ring(
        net,
        lambda o: ll_all.at[two, :, pl.ds(mult(o * 8, 8), 8), :],
        lambda o, h: ll_all.at[2 * core + h, :, pl.ds(mult(o * 8, 8), 8), :],
    )
    ring_lm = Ring(
        net,
        lambda o: lm_all.at[core, :, pl.ds(mult(o * 16, 16), 16), :],
        lambda o, h: lm_all.at[core, pl.ds(8 * h, 8), pl.ds(mult(o * 16, 16), 16), :],
    )
    ring_q = Ring(
        net,
        lambda o: q_all.at[:, :, pl.ds(mult((2 * o + core) * 128, 128), 128)],
        lambda o, h: q_all.at[pl.ds(2 * h, 2), :, pl.ds(mult((2 * o + core) * 128, 128), 128)],
    )

    for item in small:
        item.start()

    base = net.col * 256

    def lower(first, width):
        at = lambda axis: lax.broadcasted_iota(jnp.int32, (256, width), axis)
        return jnp.where(first + at(1) <= base + at(0), lr[:, pl.ds(mult(first, 128), width)], 0.0)

    left = split(jnp.transpose(lower(net.row * 512, 512)))

    @pl.loop(0, 16)
    def _(block):
        terms[lax.div(block, 4), lax.rem(block, 4)] = dot3(left, split(lower(block * 256, 256)))

    sc = TorusScatter(
        net,
        lambda o, h: terms.at[o, :, pl.ds(128 * h, 128), :],
        lambda o, h: terms.at[:, o, pl.ds(256 + 128 * h, 128), :],
        bufs_xz, bufs_zx,
    )
    sc.start()
    for item in small:
        item.first_ring()
    for item in small:
        item.first_end()
    for item in large:
        item.start()
    for a in (0, -1, 1, 2):
        for item in small:
            item.second_ring(a)
    for item in small:
        for a in (0, -1, 1, 2):
            item.second_end(a)
        item.finish()
    ring_ll.start()
    ring_lm.start()
    sc.middle()
    for item in large:
        item.first_ring()
    ring_ll.middle()
    for item in large:
        item.first_end()
    ring_ll.end()
    ring_ll.finish()
    for i in range(LOWS):
        q_own[i] = jnp.transpose(
            jnp.dot(
                jnp.transpose(p_all[i]), ll_all[i].reshape(LOW, LOW),
                preferred_element_type=F32, precision=lax.Precision.HIGHEST,
            )
        )
    local_q = pltpu.make_async_copy(q_own, ring_q.piece(y), local_sem.at[5])
    local_q.start()
    ring_lm.middle()
    for item in large:
        item.second_ring(0)
    sc.turn()
    local_q.wait()
    ring_q.start()
    for a in (-1, 1):
        for item in large:
            item.second_ring(a)
    sc.second_middle()
    for item in large:
        item.second_ring(2)
    ring_lm.end()
    ring_q.middle()
    outs = lambda base: [sigma.at[pl.ds(base + 128 * h, 128), :] for h in range(2)]
    sc.end(outs(0), outs(256))
    for item in large:
        for a in (0, -1, 1, 2):
            item.second_end(a)
        item.finish()
    ring_q.end()
    ring_lm.finish()
    ring_q.finish()
    net.finish()


def first_step(lr, m, r, p, lm, ll):
    shape = lambda *dims: jax.ShapeDtypeStruct(dims, F32)
    vmem, hbm = pl.BlockSpec(memory_space=VMEM), pl.BlockSpec(memory_space=ANY)
    return pl.pallas_call(
        first_kernel,
        out_shape=(
            shape(512, 256), shape(MIDS, MID, 512), shape(LOWS, LOW, 512), shape(LOWS, LOW, MID),
            shape(MIDS, 16, 64, MID), shape(LOWS, 16, 32, LOW),
        ),
        in_specs=[vmem] + [hbm] * 5,
        out_specs=[vmem, hbm, hbm, hbm, hbm, vmem],
        scratch_shapes=[VMEM((LOWS, LOW, 128), F32), VMEM((LOWS, LOW, 128), F32), VMEM((4, 4, 512, 256), F32)]
        + torus_bufs(128, 256) + torus_bufs(128, 256) + [
            pltpu.SemaphoreType.DMA((180,)),
            pltpu.SemaphoreType.DMA((180,)),
            pltpu.SemaphoreType.DMA((8,)),
        ],
        compiler_params=params(0),
        name="first_step",
    )(lr, m, r, p, lm, ll)


CHUNKS = 8
STEP = ROOT // 2 // CHUNKS


class Spread:
    def __init__(self, net, sources, out, send_sem, recv_sem, local_sem):
        self.net, self.sources, self.out = net, sources, out
        self.send_sem, self.recv_sem, self.local_sem = send_sem, recv_sem, local_sem
        x, z = net.place["x"], net.place["z"]
        self.lanes = pl.ds(mult(lax.rem(z, 2) * 256, 256), 256)
        self.away = lax.rem(net.place["y"] - x + 4, 4)
        self.is_core = net.place["core"] == lax.div(z, 2)

    def copy(self, way, chunk, pair):
        place = self.out.at[way, pl.ds(chunk * STEP, STEP), :]
        index = pair * 2 * CHUNKS + way * CHUNKS + chunk
        to = {"core": 1} if pair else {"y": 1 - 2 * way}
        return pltpu.make_async_remote_copy(
            src_ref=place, dst_ref=place, send_sem=self.send_sem.at[index], recv_sem=self.recv_sem.at[index],
            device_id=self.net.device(**to), device_id_type=MESH,
        )

    def load(self, way, chunk):
        per = self.sources[way].shape[1] // STEP
        source = self.sources[way].at[chunk // per, pl.ds(chunk % per * STEP, STEP), self.lanes]
        return pltpu.make_async_copy(
            source, self.out.at[way, pl.ds(chunk * STEP, STEP), :], self.local_sem.at[way * CHUNKS + chunk]
        )

    def start(self):
        @pl.when(jnp.logical_and(self.is_core, self.away == 0))
        def _():
            for chunk in range(CHUNKS):
                for way in range(2):
                    self.load(way, chunk).start()
            for chunk in range(CHUNKS):
                for way in range(2):
                    self.load(way, chunk).wait()
                    self.copy(way, chunk, 0).start()
                    self.copy(way, chunk, 1).start()

    def onward(self, first, last):
        for away in (1, 2, 3):
            @pl.when(jnp.logical_and(self.is_core, self.away == away))
            def _():
                for step in range(first, last):
                    for way in range(2):
                        hops = away if way == 0 else 4 - away
                        chunk = step + 1 - hops
                        if 0 <= chunk < CHUNKS:
                            self.copy(way, chunk, 0).wait_recv()
                            if hops < 3:
                                self.copy(way, chunk, 0).start()
                            self.copy(way, chunk, 1).start()

    def finish(self):
        for chunk in range(CHUNKS):
            for way in range(2):
                @pl.when(jnp.logical_and(self.is_core, self.away != (3, 1)[way]))
                def _():
                    self.copy(way, chunk, 0).wait_send()

                @pl.when(self.is_core)
                def _():
                    self.copy(way, chunk, 1).wait_send()

                @pl.when(jnp.logical_not(self.is_core))
                def _():
                    self.copy(way, chunk, 1).wait_recv()


def cross_kernel(cm, cl, um, ul, out_m, out_l, u_c, acc_m, acc_l, core_m, core_l, near_m, near_l, far_m, far_l,
                 send_sem, recv_sem, spread_send, spread_recv, local_sem):
    net = Net(send_sem, recv_sem)
    net.greet(("y", "core"))
    core = net.place["core"]
    other = 1 - core

    def mid_slab(y, k):
        return cm.at[:, pl.ds(mult((2 * y + k) * 128, 128), 128), :]

    def low_slab(y, k):
        return cl.at[:, pl.ds(mult((2 * y + k) * 64, 64), 64), :]

    pairs = {}
    for d in (2, 1, -1, 0):
        y = net.at("y", d)
        slot = d % 4
        pairs[d] = [
            net.send(mid_slab(y, other), core_m.at[slot], "core", 1),
            net.send(low_slab(y, other), core_l.at[slot], "core", 1),
        ]
    spread = Spread(net, (um, ul), u_c, spread_send, spread_recv, local_sem)
    spread.start()
    firsts = []
    for d in (2, 1, -1, 0):
        y = net.at("y", d)
        slot = d % 4
        for copy in pairs[d]:
            copy.wait_recv()
        acc_m[slot] = core_m[slot] + mid_slab(y, core)[...]
        acc_l[slot] = core_l[slot] + low_slab(y, core)[...]
        if d == 2:
            firsts = [net.send(acc_m.at[2], near_m, "y", 1), net.send(acc_l.at[2], near_l, "y", -1)]
    seconds = [net.send(acc_l.at[1], far_l.at[0], "y", 1), net.send(acc_m.at[3], far_m.at[1], "y", -1)]
    spread.onward(0, 1)
    firsts[0].wait_recv()
    near_m[...] += acc_m[1]
    seconds.append(net.send(near_m, far_m.at[0], "y", 1))
    firsts[1].wait_recv()
    near_l[...] += acc_l[3]
    seconds.append(net.send(near_l, far_l.at[1], "y", -1))
    spread.onward(1, CHUNKS + 2)
    for copy in seconds:
        copy.wait_recv()
    out_m[...] = acc_m[0] + far_m[0] + far_m[1]
    out_l[...] = acc_l[0] + far_l[0] + far_l[1]
    spread.finish()
    net.finish()


def cross_scatter(cm, cl, um, ul):
    vmem, hbm = pl.BlockSpec(memory_space=VMEM), pl.BlockSpec(memory_space=ANY)
    return pl.pallas_call(
        cross_kernel,
        out_shape=(
            jax.ShapeDtypeStruct((MIDS, 128, 256), F32), jax.ShapeDtypeStruct((LOWS, 64, 256), F32),
            jax.ShapeDtypeStruct((2, ROOT // 2, 256), F32),
        ),
        in_specs=[vmem, vmem, hbm, hbm],
        out_specs=[vmem] * 3,
        scratch_shapes=[
            VMEM((4, MIDS, 128, 256), F32),
            VMEM((4, LOWS, 64, 256), F32),
            VMEM((4, MIDS, 128, 256), F32),
            VMEM((4, LOWS, 64, 256), F32),
            VMEM((MIDS, 128, 256), F32),
            VMEM((LOWS, 64, 256), F32),
            VMEM((2, MIDS, 128, 256), F32),
            VMEM((2, LOWS, 64, 256), F32),
            pltpu.SemaphoreType.DMA((24,)),
            pltpu.SemaphoreType.DMA((24,)),
            pltpu.SemaphoreType.DMA((4 * CHUNKS,)),
            pltpu.SemaphoreType.DMA((4 * CHUNKS,)),
            pltpu.SemaphoreType.DMA((2 * CHUNKS,)),
        ],
        compiler_params=params(1),
        name="cross_scatter",
    )(cm, cl, um, ul)


DIAG_ROWS = 320


def diag_kernel(terms, out, *scratch):
    bufs_xz, bufs_zx, (send_sem, recv_sem) = scratch[:5], scratch[5:10], scratch[10:]
    net = Net(send_sem, recv_sem)
    net.greet(("x", "z"))
    half = DIAG_ROWS // 4

    def part_xz(o, h):
        return terms.at[o, :, pl.ds(half * h, half), :]

    def part_zx(o, h):
        return terms.at[:, o, pl.ds(2 * half + half * h, half), :]

    def outs(base):
        return [out.at[pl.ds(base + half * h, half), :] for h in range(2)]

    sc = TorusScatter(net, part_xz, part_zx, bufs_xz, bufs_zx)
    sc.start()
    sc.middle()
    sc.turn()
    sc.second_middle()
    sc.end(outs(0), outs(2 * half))
    net.finish()


def diag_scatter(terms):
    return pl.pallas_call(
        diag_kernel,
        out_shape=jax.ShapeDtypeStruct((DIAG_ROWS, 128), F32),
        in_specs=[pl.BlockSpec(memory_space=VMEM)],
        out_specs=pl.BlockSpec(memory_space=VMEM),
        scratch_shapes=torus_bufs(DIAG_ROWS // 4, 128) + torus_bufs(DIAG_ROWS // 4, 128) + [
            pltpu.SemaphoreType.DMA((32,)),
            pltpu.SemaphoreType.DMA((32,)),
        ],
        compiler_params=params(2),
        name="diag_scatter",
    )(terms)


def dot(spec, a, b):
    return jnp.einsum(spec, a, b, precision=HIGH, preferred_element_type=F32)


def lower_part(factor):
    rows_here = factor.shape[1]
    row_ids = lax.axis_index("col") * rows_here + lax.broadcasted_iota(jnp.int32, factor.shape[1:], 0)
    col_ids = lax.broadcasted_iota(jnp.int32, factor.shape[1:], 1)
    return jnp.where((col_ids <= row_ids)[None], factor, 0.0)


def live_mask(local_rows, first_row, structure, block_shift):
    row_ids = first_row + jnp.arange(local_rows, dtype=jnp.int32)
    block_ids = row_ids // BLOCK + block_shift
    return jnp.any(block_ids[None, :, None] == structure[:, None, :], axis=2).astype(F32)


def local(root_factor, mid_factor, low_factor, mid_rows, low_parent_rows, low_root_rows, mid_struct, low_struct, low_parent):
    row = lax.axis_index("row")
    lm = lower_part(mid_factor)
    ll = lower_part(low_factor)
    m = jnp.transpose(mid_rows, (0, 2, 1)) * live_mask(512, row * 512, mid_struct, 0)[:, None, :]
    r = jnp.transpose(low_root_rows, (0, 2, 1)) * live_mask(512, row * 512, low_struct, MID // BLOCK)[:, None, :]
    p = jnp.transpose(low_parent_rows, (0, 2, 1)) * live_mask(128, row * 128, low_struct, 0)[:, None, :]
    sigma, m_all, r_all, q_all, lm_all, ll_all = first_step(root_factor, m, r, p, lm, ll)
    lm_all, ll_all = lm_all.reshape(MIDS, MID, MID), ll_all.reshape(LOWS, LOW, LOW)
    ym = dot("kwj,kwa->kja", lm_all, m_all)
    yr = dot("kij,kia->kja", ll_all, r_all)
    v = jnp.stack(
        [
            yr[i] - dot("jw,wa->ja", q_all[i], lax.dynamic_index_in_dim(ym, low_parent[i], 0, keepdims=False))
            for i in range(LOWS)
        ]
    )
    cm = -dot("kja,ac->kjc", ym, sigma)
    cl = -dot("kja,ac->kjc", v, sigma)
    mid_cross, low_root, u_c = cross_scatter(cm, cl, ym, v)

    ym_c = u_c[0].reshape(MIDS, MID, 256)
    v_c = u_c[1].reshape(LOWS, LOW, 256)
    lm_v = lax.dynamic_slice_in_dim(lm, row * 128, 128, 2)
    ll_v = lax.dynamic_slice_in_dim(ll, row * 64, 64, 2)
    mid_t = dot("kcw,kcv->kwv", lm, lm_v) - dot("kwc,kvc->kwv", ym_c, mid_cross)
    low_t, par_t = [], []
    for i in range(LOWS):
        lm_p = lax.dynamic_index_in_dim(lm, low_parent[i], 0, keepdims=False)
        ym_p = lax.dynamic_index_in_dim(ym_c, low_parent[i], 0, keepdims=False)
        g = dot("jw,cw->jc", q_all[i], lm_p)
        g_v = lax.dynamic_slice_in_dim(g, row * 64, 64, 0)
        par_t.append(-(dot("wc,vc->wv", ym_p, low_root[i]) + dot("cw,vc->wv", lm_p, g_v)))
        low_t.append(
            dot("cw,cv->wv", ll[i], ll_v[i]) + dot("wc,vc->wv", g, g_v) - dot("wc,vc->wv", v_c[i], low_root[i])
        )
    pair = lambda t: [jnp.concatenate([t[0], t[1]], axis=1), jnp.concatenate([t[2], t[3]], axis=1)]
    parts = [mid_t[0].reshape(16, 64, 128), mid_t[1].reshape(16, 64, 128)]
    parts += [t.reshape(16, 64, 128) for t in pair(par_t)]
    parts += [t.reshape(16, 32, 128) for t in pair(low_t)]
    sums = diag_scatter(jnp.concatenate(parts, axis=1).reshape(4, 4, DIAG_ROWS, 128))
    mid_diag = jnp.transpose(sums[:128].reshape(2, 64, 128), (0, 2, 1))
    par = sums[128:256].reshape(2, 64, 2, 64)
    low_cross_parent = jnp.transpose(par, (0, 2, 3, 1)).reshape(4, 64, 64)
    low = sums[256:].reshape(2, 32, 2, 64)
    low_diag = jnp.transpose(low, (0, 2, 3, 1)).reshape(4, 64, 32)
    return sigma, mid_diag, mid_cross, low_diag, low_cross_parent, low_root


def solution(mesh):
    rc = P(None, "row", "col")
    in_specs = (P("col", None), P(None, "col", None), P(None, "col", None), rc, rc, rc, P(), P(), P())
    out_specs = (P("row", "col"), rc, rc, rc, rc, rc)
    return jax.shard_map(local, mesh=mesh, in_specs=in_specs, out_specs=out_specs, check_vma=False)
```

```python
import functools

import jax
import jax.numpy as jnp
from jax import lax
from jax.experimental import pallas as pl
from jax.experimental.pallas import tpu as pltpu
from jax.sharding import PartitionSpec as P

BLOCK = 256
ROOT = 4096
MID = 1024
LOW = 512
MIDS = 2
LOWS = 4
MESH = pl.DeviceIdType.MESH
F32 = jnp.float32
VMEM = pltpu.VMEM
ANY = pl.ANY


class Net:
    def __init__(self, send_sem, recv_sem):
        self.row = lax.axis_index("row")
        self.col = lax.axis_index("col")
        self.place = {
            "x": lax.div(self.col, 4),
            "z": lax.rem(self.col, 4),
            "y": lax.div(self.row, 2),
            "core": lax.rem(self.row, 2),
        }
        self.send_sem, self.recv_sem, self.used, self.started = send_sem, recv_sem, 0, []

    def at(self, axis, shift):
        if axis == "core":
            return lax.rem(self.place["core"] + shift, 2)
        return lax.rem(self.place[axis] + shift + 4, 4)

    def device(self, **shifts):
        at = {axis: self.at(axis, shifts.get(axis, 0)) for axis in self.place}
        return (at["y"] * 2 + at["core"], at["x"] * 4 + at["z"])

    def greet(self, axes):
        barrier = pltpu.get_barrier_semaphore()
        count = 0
        for axis in axes:
            for shift in (1,) if axis == "core" else (1, -1):
                pl.semaphore_signal(barrier, inc=1, device_id=self.device(**{axis: shift}), device_id_type=MESH)
                count += 1
        pl.semaphore_wait(barrier, count)

    def send(self, src, dst, axis, shift):
        index = self.used
        self.used += 1
        copy = pltpu.make_async_remote_copy(
            src_ref=src,
            dst_ref=dst,
            send_sem=self.send_sem.at[index],
            recv_sem=self.recv_sem.at[index],
            device_id=self.device(**{axis: shift}),
            device_id_type=MESH,
        )
        copy.start()
        self.started.append(copy)
        return copy

    def finish(self):
        for copy in self.started:
            copy.wait_send()


def mult(value, unit):
    return pl.multiple_of(value, unit)


def params(collective_id):
    return pltpu.CompilerParams(collective_id=collective_id, has_side_effects=True, vmem_limit_bytes=60 * 2**20)


class Gather:
    def __init__(self, net, src, dst, whole, half, first, second, local_sem, share=None):
        self.net, self.dst, self.whole, self.half = net, dst, whole, half
        self.first, self.second, self.share = first, second, share
        self.src, self.local_sem = src, local_sem

    def spot(self, a, b):
        at = {self.first: self.net.at(self.first, a), self.second: self.net.at(self.second, b)}
        return at["x"], at["z"]

    def piece(self, a, b):
        return self.whole(self.dst, *self.spot(a, b))

    def part(self, a, b, h):
        return self.half(self.dst, *self.spot(a, b), h)

    def start(self):
        net, own = self.net, self.piece(0, 0)
        self.local = pltpu.make_async_copy(self.src, own, self.local_sem)
        self.local.start()
        self.p1 = [net.send(self.src, own, self.first, s) for s in (1, -1)]
        self.p2 = {0: [net.send(self.src, own, self.second, s) for s in (1, -1)]}

    def onward(self, a):
        piece = self.piece(a, 0)
        self.p2[a] = [self.net.send(piece, piece, self.second, s) for s in (1, -1)]

    def first_ring(self):
        self.fwd = []
        for index, shift in enumerate((1, -1)):
            self.p1[index].wait_recv()
            part = self.part(-shift, 0, index)
            self.fwd.append(self.net.send(part, part, self.first, shift))
            self.onward(-shift)

    def first_end(self):
        for copy in self.fwd:
            copy.wait_recv()
        self.onward(2)

    def second_ring(self, a):
        copies = []
        for index, shift in enumerate((1, -1)):
            self.p2[a][index].wait_recv()
            part = self.part(a, -shift, index)
            copies.append(self.net.send(part, part, self.second, shift))
        self.p2[a] = copies

    def second_end(self, a):
        for copy in self.p2[a]:
            copy.wait_recv()

    def finish(self):
        self.local.wait()


class Scatter:
    def __init__(self, net, axis, part, near, far):
        self.net, self.axis, self.part, self.near, self.far = net, axis, part, near, far

    def start(self):
        opposite = self.net.at(self.axis, 2)
        self.first = [
            self.net.send(self.part(opposite, h), self.near[h], self.axis, shift) for h, shift in enumerate((1, -1))
        ]
        self.second = [
            self.net.send(self.part(self.net.at(self.axis, shift), 1 - h), self.far[h][1 - h], self.axis, shift)
            for h, shift in enumerate((1, -1))
        ]

    def middle(self):
        for h, shift in enumerate((1, -1)):
            self.first[h].wait_recv()
            self.near[h][...] += self.part(self.net.at(self.axis, shift), h)[...]
            self.second.append(self.net.send(self.near[h], self.far[h][h], self.axis, shift))

    def end(self, out):
        for copy in self.second:
            copy.wait_recv()
        for h in range(2):
            out[h][...] = self.part(self.net.at(self.axis, 0), h)[...] + self.far[0][h][...] + self.far[1][h][...]


class TorusScatter:
    def __init__(self, net, part_xz, part_zx, bufs_xz, bufs_zx):
        self.net, self.bufs = net, (bufs_xz, bufs_zx)
        self.stages = [self.stage(axis, part, bufs[0], bufs[1])
                       for axis, part, bufs in (("x", part_xz, bufs_xz), ("z", part_zx, bufs_zx))]

    def stage(self, axis, part, near, far):
        return Scatter(self.net, axis, part, [near.at[0], near.at[1]], [[far.at[s, h] for h in range(2)] for s in range(2)])

    def start(self):
        for stage in self.stages:
            stage.start()

    def middle(self):
        for stage in self.stages:
            stage.middle()

    def turn(self):
        later = []
        for stage, axis, bufs in zip(self.stages, ("z", "x"), self.bufs):
            sums = bufs[2]
            stage.end([sums.at[0], sums.at[1]])
            part = functools.partial(lambda sums, o, h: sums.at[h, o], sums)
            later.append(self.stage(axis, part, bufs[3], bufs[4]))
            later[-1].start()
        self.stages = later

    second_middle = middle

    def end(self, out_xz, out_zx):
        for stage, out in zip(self.stages, (out_xz, out_zx)):
            stage.end(out)


def torus_bufs(rows, lanes):
    return [
        VMEM((2, 4, rows, lanes), F32),
        VMEM((2, 2, 4, rows, lanes), F32),
        VMEM((2, 4, rows, lanes), F32),
        VMEM((2, rows, lanes), F32),
        VMEM((2, 2, rows, lanes), F32),
    ]


def split(a):
    high = a.astype(jnp.bfloat16)
    return high, (a - high.astype(F32)).astype(jnp.bfloat16)


def dot3(a, b):
    go = functools.partial(jnp.dot, preferred_element_type=F32)
    return go(a[0], b[0]) + (go(a[0], b[1]) + go(a[1], b[0]))


class Ring:
    def __init__(self, net, pieces, halves):
        self.net, self.pieces, self.halves = net, pieces, halves

    def pair_up(self, place):
        self.pair += [self.net.send(part, part, "core", 1) for part in self.pieces(place)]

    def start(self):
        own = self.pieces(self.net.at("y", 0))
        self.near = [[self.net.send(part, part, "y", s) for part in own] for s in (1, -1)]
        self.pair = []
        self.pair_up(self.net.at("y", 0))

    def middle(self):
        self.far = []
        for index, shift in enumerate((1, -1)):
            for copy in self.near[index]:
                copy.wait_recv()
            place = self.net.at("y", -shift)
            self.far += [self.net.send(part, part, "y", shift) for part in self.halves(place, index)]
            self.pair_up(place)

    def end(self):
        for copy in self.far:
            copy.wait_recv()
        self.pair_up(self.net.at("y", 2))

    def finish(self):
        for copy in self.pair:
            copy.wait_recv()


def first_kernel(lr, m, r, p, lm, ll, sigma, m_all, r_all, q_all, lm_all, ll_all, p_all, q_own, terms, *scratch):
    bufs_xz, bufs_zx, (send_sem, recv_sem, local_sem) = scratch[:5], scratch[5:10], scratch[10:]
    net = Net(send_sem, recv_sem)
    net.greet(("x", "z", "y", "core"))
    core, y = net.place["core"], net.place["y"]

    def rows(x, z, n):
        return pl.ds(mult((x * 4 + z) * n, n), n)

    def eighth(n):
        return pl.ds(mult(y * n, n), n)

    two = pl.ds(2 * core, 2)
    ga_p = Gather(
        net, p, p_all,
        lambda ref, x, z: ref.at[:, rows(x, z, 32), :],
        lambda ref, x, z, h: ref.at[pl.ds(2 * h, 2), rows(x, z, 32), :],
        "x", "z", local_sem.at[0],
    )
    ga_ll = Gather(
        net, ll.at[two, eighth(8), :], ll_all,
        lambda ref, x, z: ref.at[two, x * 4 + z, eighth(8), :],
        lambda ref, x, z, h: ref.at[2 * core + h, x * 4 + z, eighth(8), :],
        "z", "x", local_sem.at[1],
    )
    ga_lm = Gather(
        net, lm.at[core, eighth(16), :], lm_all,
        lambda ref, x, z: ref.at[core, x * 4 + z, eighth(16), :],
        lambda ref, x, z, h: ref.at[core, x * 4 + z, pl.ds(mult(y * 16 + 8 * h, 8), 8), :],
        "x", "z", local_sem.at[2],
    )
    ga_m = Gather(
        net, m, m_all,
        lambda ref, x, z: ref.at[:, rows(x, z, 64), :],
        lambda ref, x, z, h: ref.at[h, rows(x, z, 64), :],
        "x", "z", local_sem.at[3],
    )
    ga_r = Gather(
        net, r, r_all,
        lambda ref, x, z: ref.at[:, rows(x, z, 32), :],
        lambda ref, x, z, h: ref.at[pl.ds(2 * h, 2), rows(x, z, 32), :],
        "z", "x", local_sem.at[4],
    )
    small, large = (ga_p, ga_ll, ga_lm), (ga_m, ga_r)
    def ll_parts(o):
        return [ll_all.at[two, pl.ds(8 * g, 8), pl.ds(mult(o * 8, 8), 8), pl.ds(0, 256 * (g + 1))] for g in range(2)]

    def lm_parts(o):
        return [
            lm_all.at[core, pl.ds(4 * g, 4), pl.ds(mult(o * 16, 16), 16), pl.ds(0, 256 * (g + 1))] for g in range(4)
        ]

    def q_lanes(o):
        return pl.ds(mult((2 * o + core) * 128, 128), 128)

    ring_ll = Ring(net, ll_parts, lambda o, h: ll_parts(o)[1:] if h else ll_parts(o)[:1])
    ring_lm = Ring(net, lm_parts, lambda o, h: lm_parts(o)[:3] if h else lm_parts(o)[3:])
    ring_q = Ring(net, lambda o: [q_all.at[:, :, q_lanes(o)]], lambda o, h: [q_all.at[pl.ds(2 * h, 2), :, q_lanes(o)]])

    for item in small + large:
        item.start()

    base = net.col * 256

    def lower(first, width):
        at = lambda axis: lax.broadcasted_iota(jnp.int32, (256, width), axis)
        return jnp.where(first + at(1) <= base + at(0), lr[:, pl.ds(mult(first, 128), width)], 0.0)

    left = split(jnp.transpose(lower(net.row * 512, 512)))

    @pl.loop(0, 16)
    def _(block):
        terms[lax.div(block, 4), lax.rem(block, 4)] = dot3(left, split(lower(block * 256, 256)))

    sc = TorusScatter(
        net,
        lambda o, h: terms.at[o, :, pl.ds(128 * h, 128), :],
        lambda o, h: terms.at[:, o, pl.ds(256 + 128 * h, 128), :],
        bufs_xz, bufs_zx,
    )
    sc.start()
    for item in small:
        item.first_ring()
    for item in small:
        item.first_end()
    for a in (0, -1, 1, 2):
        for item in small:
            item.second_ring(a)
    for item in large:
        item.first_ring()
    for item in small:
        for a in (0, -1, 1, 2):
            item.second_end(a)
        item.finish()
    ring_ll.start()
    ring_lm.start()
    for item in large:
        item.first_end()
    sc.middle()
    ring_ll.middle()
    for item in large:
        item.second_ring(0)
    ring_ll.end()
    ring_ll.finish()
    exact = functools.partial(jnp.dot, preferred_element_type=F32, precision=lax.Precision.HIGHEST)
    for i in range(LOWS):
        pt = jnp.transpose(p_all[i])
        q_own[i, :256] = jnp.transpose(exact(pt, ll_all[i, :, :, :256].reshape(LOW, 256)))
        q_own[i, 256:] = jnp.transpose(exact(pt[:, 256:], ll_all[i, 8:, :, 256:].reshape(256, 256)))
    local_q = pltpu.make_async_copy(q_own, q_all.at[:, :, q_lanes(y)], local_sem.at[5])
    local_q.start()
    for a in (-1, 1):
        for item in large:
            item.second_ring(a)
    local_q.wait()
    ring_q.start()
    sc.turn()
    ring_lm.middle()
    for item in large:
        item.second_ring(2)
    sc.second_middle()
    ring_q.middle()
    ring_lm.end()
    outs = lambda base: [sigma.at[pl.ds(base + 128 * h, 128), :] for h in range(2)]
    sc.end(outs(0), outs(256))
    for item in large:
        for a in (0, -1, 1, 2):
            item.second_end(a)
        item.finish()
    ring_q.end()
    ring_lm.finish()
    ring_q.finish()
    net.finish()


def first_step(lr, m, r, p, lm, ll):
    shape = lambda *dims: jax.ShapeDtypeStruct(dims, F32)
    vmem, hbm = pl.BlockSpec(memory_space=VMEM), pl.BlockSpec(memory_space=ANY)
    return pl.pallas_call(
        first_kernel,
        out_shape=(
            shape(512, 256), shape(MIDS, MID, 512), shape(LOWS, LOW, 512), shape(LOWS, LOW, MID),
            shape(MIDS, 16, 64, MID), shape(LOWS, 16, 32, LOW),
        ),
        in_specs=[vmem] + [hbm] * 5,
        out_specs=[vmem, hbm, hbm, hbm, hbm, vmem],
        scratch_shapes=[VMEM((LOWS, LOW, 128), F32), VMEM((LOWS, LOW, 128), F32), VMEM((4, 4, 512, 256), F32)]
        + torus_bufs(128, 256) + torus_bufs(128, 256) + [
            pltpu.SemaphoreType.DMA((220,)),
            pltpu.SemaphoreType.DMA((220,)),
            pltpu.SemaphoreType.DMA((8,)),
        ],
        compiler_params=params(0),
        name="first_step",
    )(lr, m, r, p, lm, ll)


CHUNKS = 4
STEP = 256


class Spread:
    def __init__(self, net, source, out, send_sem, recv_sem, local_sem):
        self.net, self.source, self.out = net, source, out
        self.send_sem, self.recv_sem, self.local_sem = send_sem, recv_sem, local_sem
        x, z = net.place["x"], net.place["z"]
        self.lanes = pl.ds(mult(lax.rem(z, 2) * 256, 256), 256)
        self.away = lax.rem(net.place["y"] - x + 4, 4)
        self.is_core = net.place["core"] == lax.div(z, 2)

    def spot(self, ref, way, chunk, lanes):
        per = ref.shape[1] // STEP
        return ref.at[way * (ref.shape[0] // 2) + chunk // per, pl.ds(chunk % per * STEP, STEP), lanes]

    def copy(self, way, chunk, pair, first=False):
        place = self.spot(self.out, way, chunk, slice(None))
        index = pair * 2 * CHUNKS + way * CHUNKS + chunk
        to = {"core": 1} if pair else {"y": 1 - 2 * way}
        return pltpu.make_async_remote_copy(
            src_ref=self.spot(self.source, way, chunk, self.lanes) if first else place, dst_ref=place,
            send_sem=self.send_sem.at[index], recv_sem=self.recv_sem.at[index],
            device_id=self.net.device(**to), device_id_type=MESH,
        )

    def load(self):
        return pltpu.make_async_copy(self.source.at[:, :, self.lanes], self.out, self.local_sem)

    def start(self):
        @pl.when(jnp.logical_and(self.is_core, self.away == 0))
        def _():
            self.load().start()
            for chunk in range(CHUNKS):
                for way in range(2):
                    self.copy(way, chunk, 0, True).start()
            for chunk in range(CHUNKS):
                for way in range(2):
                    self.copy(way, chunk, 1, True).start()

    def onward(self, first, last):
        for away in (1, 2, 3):
            @pl.when(jnp.logical_and(self.is_core, self.away == away))
            def _():
                for step in range(first, last):
                    for way in range(2):
                        hops = away if way == 0 else 4 - away
                        chunk = step + 1 - hops
                        if 0 <= chunk < CHUNKS:
                            self.copy(way, chunk, 0).wait_recv()
                            if hops < 3:
                                self.copy(way, chunk, 0).start()
                            self.copy(way, chunk, 1).start()

    def finish(self):
        @pl.when(jnp.logical_and(self.is_core, self.away == 0))
        def _():
            self.load().wait()

        for chunk in range(CHUNKS):
            for way in range(2):
                @pl.when(jnp.logical_and(self.is_core, self.away != (3, 1)[way]))
                def _():
                    self.copy(way, chunk, 0).wait_send()

                @pl.when(self.is_core)
                def _():
                    self.copy(way, chunk, 1).wait_send()

                @pl.when(jnp.logical_not(self.is_core))
                def _():
                    self.copy(way, chunk, 1).wait_recv()


def dot3_nt(a, b):
    go = lambda s, t: lax.dot_general(s, t, (((1,), (1,)), ((), ())), preferred_element_type=F32)
    return go(a[0], b[0]) + (go(a[0], b[1]) + go(a[1], b[0]))


def second_kernel(parent, sigma, lm_own, m_all, r_all, q_all, lm_all, ll_all, out_m, out_l, um_c, ul_c, g,
                  m, r, q, lm, ll, high, low, s_high, s_low, cm, cl, acc_m, acc_l, core_m, core_l, near_m, near_l,
                  far_m, far_l, send_sem, recv_sem, spread_send, spread_recv, local_sem):
    loads = [
        pltpu.make_async_copy(src, dst, local_sem.at[index])
        for index, (src, dst) in enumerate(((lm_all, lm), (m_all, m), (ll_all, ll), (r_all, r), (q_all, q)))
    ]
    for load in loads:
        load.start()
    net = Net(send_sem, recv_sem)
    net.greet(("y", "core"))
    core = net.place["core"]
    other = 1 - core
    s_high[...], s_low[...] = split(sigma[...])
    halves = lambda: (s_high[...], s_low[...])

    def band(block):
        return pl.ds(block * 256, 256)

    loads[0].wait()
    loads[1].wait()

    @pl.loop(0, MIDS)
    def _(p):
        for j in range(4):
            total = None
            for k in range(j, 4):
                tile = jnp.transpose(lm[p, pl.ds(4 * k, 4), :, band(j)].reshape(256, 256))
                term = dot3(split(tile), split(m[p, band(k), :]))
                total = term if total is None else total + term
            m[p, band(j), :] = total
            both = split(total)
            high[p, band(j), :], low[p, band(j), :] = both
            cm[p, band(j), :] = -dot3(both, halves())

    def slab(ref, rows, y, k):
        return ref.at[:, pl.ds(mult((2 * y + k) * rows, rows), rows), :]

    pair_m = {d: net.send(slab(cm, 128, net.at("y", d), other), core_m.at[d % 4], "core", 1) for d in (2, 1, -1, 0)}
    spread_m = Spread(net, m, um_c, spread_send.at[0], spread_recv.at[0], local_sem.at[5])
    spread_m.start()
    for load in loads[2:]:
        load.wait()

    def low_nodes(first):
        @pl.loop(first, first + 2)
        def _(i):
            p = parent[i]
            own = split(lm_own[p])
            for j in range(2):
                total = None
                for k in range(j, 2):
                    tile = jnp.transpose(ll[i, pl.ds(8 * k, 8), :, band(j)].reshape(256, 256))
                    term = dot3(split(tile), split(r[i, band(k), :]))
                    total = term if total is None else total + term
                q_both = split(q[i, band(j), :])
                total = total - dot3(q_both, (high[p], low[p]))
                g[i, band(j), :] = dot3_nt(q_both, own)
                r[i, band(j), :] = total
                cl[i, band(j), :] = -dot3(split(total), halves())

    low_nodes(0)
    spread_m.onward(0, 3)
    low_nodes(2)
    pair_l = {d: net.send(slab(cl, 64, net.at("y", d), other), core_l.at[d % 4], "core", 1) for d in (2, 1, -1, 0)}
    spread_m.onward(3, CHUNKS + 2)
    firsts = []
    spread_l = Spread(net, r, ul_c, spread_send.at[1], spread_recv.at[1], local_sem.at[6])
    for d in (2, 1, -1, 0):
        y = net.at("y", d)
        slot = d % 4
        pair_m[d].wait_recv()
        acc_m[slot] = core_m[slot] + slab(cm, 128, y, core)[...]
        pair_l[d].wait_recv()
        acc_l[slot] = core_l[slot] + slab(cl, 64, y, core)[...]
        if d == 2:
            firsts = [net.send(acc_m.at[2], near_m, "y", 1), net.send(acc_l.at[2], near_l, "y", -1)]
    seconds = [net.send(acc_l.at[1], far_l.at[0], "y", 1), net.send(acc_m.at[3], far_m.at[1], "y", -1)]
    spread_l.start()
    firsts[0].wait_recv()
    near_m[...] += acc_m[1]
    seconds.append(net.send(near_m, far_m.at[0], "y", 1))
    firsts[1].wait_recv()
    near_l[...] += acc_l[3]
    seconds.append(net.send(near_l, far_l.at[1], "y", -1))
    spread_l.onward(0, CHUNKS + 2)
    for copy in seconds:
        copy.wait_recv()
    out_m[...] = acc_m[0] + far_m[0] + far_m[1]
    out_l[...] = acc_l[0] + far_l[0] + far_l[1]
    spread_m.finish()
    spread_l.finish()
    net.finish()


def second_step(parent, sigma, lm, m_all, r_all, q_all, lm_all, ll_all):
    shape = lambda *dims: jax.ShapeDtypeStruct(dims, F32)
    vmem, hbm = pl.BlockSpec(memory_space=VMEM), pl.BlockSpec(memory_space=ANY)
    block = lambda *dims: VMEM(dims, F32)
    half = lambda *dims: VMEM(dims, jnp.bfloat16)
    return pl.pallas_call(
        second_kernel,
        out_shape=(
            shape(MIDS, 128, 256), shape(LOWS, 64, 256), shape(MIDS, MID, 256), shape(LOWS, LOW, 256), shape(LOWS, LOW, 64),
        ),
        in_specs=[pl.BlockSpec(memory_space=pltpu.SMEM), vmem, vmem] + [hbm] * 5,
        out_specs=[vmem] * 5,
        scratch_shapes=[
            block(MIDS, MID, 512), block(LOWS, LOW, 512), block(LOWS, LOW, MID), block(MIDS, 16, 64, MID),
            block(LOWS, 16, 32, LOW), half(MIDS, MID, 512), half(MIDS, MID, 512), half(512, 256), half(512, 256),
            block(MIDS, MID, 256), block(LOWS, LOW, 256),
            block(4, MIDS, 128, 256), block(4, LOWS, 64, 256), block(4, MIDS, 128, 256), block(4, LOWS, 64, 256),
            block(MIDS, 128, 256), block(LOWS, 64, 256), block(2, MIDS, 128, 256), block(2, LOWS, 64, 256),
            pltpu.SemaphoreType.DMA((24,)),
            pltpu.SemaphoreType.DMA((24,)),
            pltpu.SemaphoreType.DMA((2, 4 * CHUNKS)),
            pltpu.SemaphoreType.DMA((2, 4 * CHUNKS)),
            pltpu.SemaphoreType.DMA((8,)),
        ],
        compiler_params=params(1),
        name="second_step",
    )(parent, sigma, lm, m_all, r_all, q_all, lm_all, ll_all)


DIAG_ROWS = 320


def third_kernel(parent, mid_cross, low_root, um, ul, g, lm, ll, out, terms, lm_t, ll_t, *scratch):
    bufs_xz, bufs_zx, (send_sem, recv_sem) = scratch[:5], scratch[5:10], scratch[10:]
    net = Net(send_sem, recv_sem)
    net.greet(("x", "z"))
    for p in range(MIDS):
        lm_t[p] = jnp.transpose(lm[p])
    for i in range(LOWS):
        ll_t[i] = jnp.transpose(ll[i])
    low_rows = pl.ds(mult(net.row * 64, 64), 64)
    for p in range(MIDS):
        mine = split(lm_t[p, pl.ds(mult(net.row * 128, 128), 128), :])
        term = dot3_nt(split(lm_t[p]), mine) - dot3_nt(split(um[p]), split(mid_cross[p]))
        terms[:, :, pl.ds(64 * p, 64), :] = term.reshape(4, 4, 64, 128)
    for pair in range(2):
        par, own = [], []
        for i in (2 * pair, 2 * pair + 1):
            p = parent[i]
            root, g_mine = split(low_root[i]), split(g[i, low_rows, :])
            par.append(-(dot3_nt(split(um[p]), root) + dot3_nt(split(lm_t[p]), g_mine)))
            own.append(
                dot3_nt(split(ll_t[i]), split(ll_t[i, low_rows, :])) + dot3_nt(split(g[i]), g_mine)
                - dot3_nt(split(ul[i]), root)
            )
        terms[:, :, pl.ds(128 + 64 * pair, 64), :] = jnp.concatenate(par, axis=1).reshape(4, 4, 64, 128)
        terms[:, :, pl.ds(256 + 32 * pair, 32), :] = jnp.concatenate(own, axis=1).reshape(4, 4, 32, 128)
    half = DIAG_ROWS // 4

    def outs(base):
        return [out.at[pl.ds(base + half * h, half), :] for h in range(2)]

    sc = TorusScatter(
        net,
        lambda o, h: terms.at[o, :, pl.ds(half * h, half), :],
        lambda o, h: terms.at[:, o, pl.ds(2 * half + half * h, half), :],
        bufs_xz, bufs_zx,
    )
    sc.start()
    sc.middle()
    sc.turn()
    sc.second_middle()
    sc.end(outs(0), outs(2 * half))
    net.finish()


def third_step(parent, *arrays):
    return pl.pallas_call(
        third_kernel,
        out_shape=jax.ShapeDtypeStruct((DIAG_ROWS, 128), F32),
        in_specs=[pl.BlockSpec(memory_space=pltpu.SMEM)] + [pl.BlockSpec(memory_space=VMEM)] * 7,
        out_specs=pl.BlockSpec(memory_space=VMEM),
        scratch_shapes=[
            VMEM((4, 4, DIAG_ROWS, 128), F32), VMEM((MIDS, MID, 64), F32), VMEM((LOWS, LOW, 32), F32),
        ] + torus_bufs(DIAG_ROWS // 4, 128) + torus_bufs(DIAG_ROWS // 4, 128) + [
            pltpu.SemaphoreType.DMA((32,)),
            pltpu.SemaphoreType.DMA((32,)),
        ],
        compiler_params=params(2),
        name="third_step",
    )(parent, *arrays)


def lower_part(factor):
    rows_here = factor.shape[1]
    row_ids = lax.axis_index("col") * rows_here + lax.broadcasted_iota(jnp.int32, factor.shape[1:], 0)
    col_ids = lax.broadcasted_iota(jnp.int32, factor.shape[1:], 1)
    return jnp.where((col_ids <= row_ids)[None], factor, 0.0)


def live_mask(local_rows, first_row, structure, block_shift):
    row_ids = first_row + jnp.arange(local_rows, dtype=jnp.int32)
    block_ids = row_ids // BLOCK + block_shift
    return jnp.any(block_ids[None, :, None] == structure[:, None, :], axis=2).astype(F32)


def local(root_factor, mid_factor, low_factor, mid_rows, low_parent_rows, low_root_rows, mid_struct, low_struct, low_parent):
    row = lax.axis_index("row")
    lm = lower_part(mid_factor)
    ll = lower_part(low_factor)
    m = jnp.transpose(mid_rows, (0, 2, 1)) * live_mask(512, row * 512, mid_struct, 0)[:, None, :]
    r = jnp.transpose(low_root_rows, (0, 2, 1)) * live_mask(512, row * 512, low_struct, MID // BLOCK)[:, None, :]
    p = jnp.transpose(low_parent_rows, (0, 2, 1)) * live_mask(128, row * 128, low_struct, 0)[:, None, :]
    sigma, m_all, r_all, q_all, lm_all, ll_all = first_step(root_factor, m, r, p, lm, ll)
    mid_cross, low_root, um_c, ul_c, g = second_step(low_parent, sigma, lm, m_all, r_all, q_all, lm_all, ll_all)
    sums = third_step(low_parent, mid_cross, low_root, um_c, ul_c, g, lm, ll)
    mid_diag = jnp.transpose(sums[:128].reshape(2, 64, 128), (0, 2, 1))
    par = sums[128:256].reshape(2, 64, 2, 64)
    low_cross_parent = jnp.transpose(par, (0, 2, 3, 1)).reshape(4, 64, 64)
    low = sums[256:].reshape(2, 32, 2, 64)
    low_diag = jnp.transpose(low, (0, 2, 3, 1)).reshape(4, 64, 32)
    return sigma, mid_diag, mid_cross, low_diag, low_cross_parent, low_root


def solution(mesh):
    rc = P(None, "row", "col")
    in_specs = (P("col", None), P(None, "col", None), P(None, "col", None), rc, rc, rc, P(), P(), P())
    out_specs = (P("row", "col"), rc, rc, rc, rc, rc)
    return jax.shard_map(local, mesh=mesh, in_specs=in_specs, out_specs=out_specs, check_vma=False)
```

```python
import functools

import jax
import jax.numpy as jnp
from jax import lax
from jax.experimental import pallas as pl
from jax.experimental.pallas import tpu as pltpu
from jax.sharding import PartitionSpec as P

BLOCK = 256
ROOT = 4096
MID = 1024
LOW = 512
MIDS = 2
LOWS = 4
MESH = pl.DeviceIdType.MESH
F32 = jnp.float32
VMEM = pltpu.VMEM
ANY = pl.ANY


class Net:
    def __init__(self, send_sem, recv_sem):
        self.row = lax.axis_index("row")
        self.col = lax.axis_index("col")
        self.place = {
            "x": lax.div(self.col, 4),
            "z": lax.rem(self.col, 4),
            "y": lax.div(self.row, 2),
            "core": lax.rem(self.row, 2),
        }
        self.send_sem, self.recv_sem, self.used, self.started = send_sem, recv_sem, 0, []

    def at(self, axis, shift):
        if axis == "core":
            return lax.rem(self.place["core"] + shift, 2)
        return lax.rem(self.place[axis] + shift + 4, 4)

    def device(self, **shifts):
        at = {axis: self.at(axis, shifts.get(axis, 0)) for axis in self.place}
        return (at["y"] * 2 + at["core"], at["x"] * 4 + at["z"])

    def greet(self, axes):
        barrier = pltpu.get_barrier_semaphore()
        count = 0
        for axis in axes:
            for shift in (1,) if axis == "core" else (1, -1):
                pl.semaphore_signal(barrier, inc=1, device_id=self.device(**{axis: shift}), device_id_type=MESH)
                count += 1
        pl.semaphore_wait(barrier, count)

    def send(self, src, dst, axis, shift):
        index = self.used
        self.used += 1
        copy = pltpu.make_async_remote_copy(
            src_ref=src,
            dst_ref=dst,
            send_sem=self.send_sem.at[index],
            recv_sem=self.recv_sem.at[index],
            device_id=self.device(**{axis: shift}),
            device_id_type=MESH,
        )
        copy.start()
        self.started.append(copy)
        return copy

    def finish(self):
        for copy in self.started:
            copy.wait_send()


def mult(value, unit):
    return pl.multiple_of(value, unit)


def params(collective_id):
    return pltpu.CompilerParams(collective_id=collective_id, has_side_effects=True, vmem_limit_bytes=62 * 2**20)


class Gather:
    def __init__(self, net, src, dst, whole, half, first, second, local_sem, share=None):
        self.net, self.dst, self.whole, self.half = net, dst, whole, half
        self.first, self.second, self.share = first, second, share
        self.src, self.local_sem, self.sent = src, local_sem, []

    def send(self, *args):
        copy = self.net.send(*args)
        self.sent.append(copy)
        return copy

    def free(self):
        for copy in self.sent:
            copy.wait_send()
        self.net.started = [copy for copy in self.net.started if not any(copy is one for one in self.sent)]

    def spot(self, a, b):
        at = {self.first: self.net.at(self.first, a), self.second: self.net.at(self.second, b)}
        return at["x"], at["z"]

    def piece(self, a, b):
        return self.whole(self.dst, *self.spot(a, b))

    def part(self, a, b, h):
        return self.half(self.dst, *self.spot(a, b), h)

    def start(self):
        net, own = self.net, self.piece(0, 0)
        self.local = pltpu.make_async_copy(self.src, own, self.local_sem)
        self.local.start()
        self.p1 = [self.send(self.src, own, self.first, s) for s in (1, -1)]
        self.p2 = {0: [self.send(self.src, own, self.second, s) for s in (1, -1)]}

    def onward(self, a):
        piece = self.piece(a, 0)
        self.p2[a] = [self.send(piece, piece, self.second, s) for s in (1, -1)]

    def first_ring(self):
        self.fwd = []
        for index, shift in enumerate((1, -1)):
            self.p1[index].wait_recv()
            part = self.part(-shift, 0, index)
            self.fwd.append(self.send(part, part, self.first, shift))
            self.onward(-shift)

    def first_end(self):
        for copy in self.fwd:
            copy.wait_recv()
        self.onward(2)

    def second_ring(self, a):
        copies = []
        for index, shift in enumerate((1, -1)):
            self.p2[a][index].wait_recv()
            part = self.part(a, -shift, index)
            copies.append(self.send(part, part, self.second, shift))
        self.p2[a] = copies

    def second_end(self, a):
        for copy in self.p2[a]:
            copy.wait_recv()

    def finish(self):
        self.local.wait()


class Scatter:
    def __init__(self, net, axis, part, near, far):
        self.net, self.axis, self.part, self.near, self.far = net, axis, part, near, far

    def start(self):
        opposite = self.net.at(self.axis, 2)
        self.first = [
            self.net.send(self.part(opposite, h), self.near[h], self.axis, shift) for h, shift in enumerate((1, -1))
        ]

    def plain(self):
        self.second = [
            self.net.send(self.part(self.net.at(self.axis, shift), 1 - h), self.far[h][1 - h], self.axis, shift)
            for h, shift in enumerate((1, -1))
        ]

    def middle(self):
        for h, shift in enumerate((1, -1)):
            self.first[h].wait_recv()
            self.near[h][...] += self.part(self.net.at(self.axis, shift), h)[...]
            self.second.append(self.net.send(self.near[h], self.far[h][h], self.axis, shift))

    def end(self, out):
        for copy in self.second:
            copy.wait_recv()
        for h in range(2):
            out[h][...] = self.part(self.net.at(self.axis, 0), h)[...] + self.far[0][h][...] + self.far[1][h][...]


class TorusScatter:
    def __init__(self, net, part_xz, part_zx, bufs_xz, bufs_zx):
        self.net, self.bufs = net, (bufs_xz, bufs_zx)
        self.stages = [self.stage(axis, part, bufs[0], bufs[1])
                       for axis, part, bufs in (("x", part_xz, bufs_xz), ("z", part_zx, bufs_zx))]

    def stage(self, axis, part, near, far):
        return Scatter(self.net, axis, part, [near.at[0], near.at[1]], [[far.at[s, h] for h in range(2)] for s in range(2)])

    def start(self):
        for stage in self.stages:
            stage.start()

    def plain(self):
        for stage in self.stages:
            stage.plain()

    def middle(self):
        for stage in self.stages:
            stage.middle()

    def turn(self):
        later = []
        for stage, axis, bufs in zip(self.stages, ("z", "x"), self.bufs):
            sums = bufs[2]
            stage.end([sums.at[0], sums.at[1]])
            part = functools.partial(lambda sums, o, h: sums.at[h, o], sums)
            later.append(self.stage(axis, part, bufs[3], bufs[4]))
            later[-1].start()
            later[-1].plain()
        self.stages = later

    second_middle = middle

    def end(self, out_xz, out_zx):
        for stage, out in zip(self.stages, (out_xz, out_zx)):
            stage.end(out)


def torus_bufs(rows, lanes):
    return [
        VMEM((2, 4, rows, lanes), F32),
        VMEM((2, 2, 4, rows, lanes), F32),
        VMEM((2, 4, rows, lanes), F32),
        VMEM((2, rows, lanes), F32),
        VMEM((2, 2, rows, lanes), F32),
    ]


def split(a):
    high = a.astype(jnp.bfloat16)
    return high, (a - high.astype(F32)).astype(jnp.bfloat16)


def dot3(a, b):
    go = functools.partial(jnp.dot, preferred_element_type=F32)
    return go(a[0], b[0]) + (go(a[0], b[1]) + go(a[1], b[0]))


class Ring:
    def __init__(self, net, pieces, halves, share=True):
        self.net, self.pieces, self.halves, self.share = net, pieces, halves, share

    def pair_up(self, place):
        if self.share:
            self.pair += [self.net.send(part, part, "core", 1) for part in self.pieces(place)]

    def start(self):
        own = self.pieces(self.net.at("y", 0))
        self.near = [[self.net.send(part, part, "y", s) for part in own] for s in (1, -1)]
        self.pair = []
        self.pair_up(self.net.at("y", 0))

    def middle(self):
        self.far = []
        for index, shift in enumerate((1, -1)):
            for copy in self.near[index]:
                copy.wait_recv()
            place = self.net.at("y", -shift)
            self.far += [self.net.send(part, part, "y", shift) for part in self.halves(place, index)]
            self.pair_up(place)

    def end(self):
        for copy in self.far:
            copy.wait_recv()
        self.pair_up(self.net.at("y", 2))

    def finish(self):
        for copy in self.pair:
            copy.wait_recv()


CHUNKS = 4
STEP = 256


class Spread:
    def __init__(self, net, source, out, send_sem, recv_sem, local_sem):
        self.net, self.source, self.out = net, source, out
        self.send_sem, self.recv_sem, self.local_sem = send_sem, recv_sem, local_sem
        x, z = net.place["x"], net.place["z"]
        self.lanes = pl.ds(mult(lax.rem(z, 2) * 256, 256), 256)
        self.away = lax.rem(net.place["y"] - x + 4, 4)
        self.is_core = net.place["core"] == lax.div(z, 2)

    def spot(self, ref, way, chunk, lanes):
        per = ref.shape[1] // STEP
        return ref.at[way * (ref.shape[0] // 2) + chunk // per, pl.ds(chunk % per * STEP, STEP), lanes]

    def copy(self, way, chunk, pair):
        place = self.spot(self.out, way, chunk, slice(None))
        index = pair * 2 * CHUNKS + way * CHUNKS + chunk
        to = {"core": 1} if pair else {"y": 1 - 2 * way}
        return pltpu.make_async_remote_copy(
            src_ref=place, dst_ref=place,
            send_sem=self.send_sem.at[index], recv_sem=self.recv_sem.at[index],
            device_id=self.net.device(**to), device_id_type=MESH,
        )

    def load(self):
        return pltpu.make_async_copy(self.source.at[:, :, self.lanes], self.out, self.local_sem)

    def start(self):
        @pl.when(jnp.logical_and(self.is_core, self.away == 0))
        def _():
            self.load().start()
            self.load().wait()
            for pair in range(2):
                for chunk in range(CHUNKS):
                    for way in range(2):
                        self.copy(way, chunk, pair).start()

    def onward(self, first, last):
        for away in (1, 2, 3):
            @pl.when(jnp.logical_and(self.is_core, self.away == away))
            def _():
                for step in range(first, last):
                    for way in range(2):
                        hops = away if way == 0 else 4 - away
                        chunk = step + 1 - hops
                        if 0 <= chunk < CHUNKS:
                            self.copy(way, chunk, 0).wait_recv()
                            if hops < 3:
                                self.copy(way, chunk, 0).start()
                            self.copy(way, chunk, 1).start()

    def finish(self):
        for chunk in range(CHUNKS):
            for way in range(2):
                @pl.when(jnp.logical_and(self.is_core, self.away != (3, 1)[way]))
                def _():
                    self.copy(way, chunk, 0).wait_send()

                @pl.when(self.is_core)
                def _():
                    self.copy(way, chunk, 1).wait_send()

                @pl.when(jnp.logical_not(self.is_core))
                def _():
                    self.copy(way, chunk, 1).wait_recv()


def dot3_nt(a, b):
    go = lambda s, t: lax.dot_general(s, t, (((1,), (1,)), ((), ())), preferred_element_type=F32)
    return go(a[0], b[0]) + (go(a[0], b[1]) + go(a[1], b[0]))


def main_kernel(parent, lr, lm_own, m, r, p, ll, sigma, out_m, out_l, g, um_c, ul_c, lm_all, p_all,
                m_all, r_all, p_mine, g_in, ll_all, stage, high, low, s_high, s_low, terms, cm, cl,
                acc_m, acc_l, core_m, core_l, near_m, near_l, far_m, far_l, *scratch):
    bufs_xz, bufs_zx, (send_sem, recv_sem, spread_send, spread_recv, local_sem, load_sem) = (
        scratch[:5], scratch[5:10], scratch[10:]
    )
    net = Net(send_sem, recv_sem)
    core, y = net.place["core"], net.place["y"]
    other = 1 - core

    def band(block):
        return pl.ds(block * 256, 256)

    def root_block(b):
        return cm.at[b // 4, band(b % 4), :] if b < 8 else cl.at[(b - 8) // 2, band(b % 2), :]

    root_loads = [
        pltpu.make_async_copy(
            lr.at[pl.ds(128 * t, 128), pl.ds(mult(net.row * 512 + 256 * h, 256), 256)], acc_m.at[h, t], load_sem.at[2 * h + t]
        )
        for h in range(2)
        for t in range(2)
    ]
    root_loads += [pltpu.make_async_copy(lr.at[:, band(b)], root_block(b), load_sem.at[4 + b]) for b in range(16)]
    for load in root_loads:
        load.start()
    net.greet(("x", "z", "y", "core"))

    def rows(x, z, n):
        return pl.ds(mult((x * 4 + z) * n, n), n)

    def eighth(n):
        return pl.ds(mult(y * n, n), n)

    two = pl.ds(2 * core, 2)
    def p_lanes(o):
        return pl.ds(mult(o * 256, 256), 256)

    ring_p = Ring(net, lambda o: [p_mine.at[:, :, p_lanes(o)]], lambda o, h: [p_mine.at[h, :, p_lanes(o)]], share=False)
    ga_ps = tuple(
        Gather(
            net, p_mine.at[h], p_all,
            lambda ref, x, z, h=h: ref.at[2 * core + h, rows(x, z, 32), :],
            lambda ref, x, z, part, h=h: ref.at[2 * core + h, pl.ds(mult((x * 4 + z) * 32 + 16 * part, 16), 16), :],
            first, second, local_sem.at[(0, 5)[h]],
        )
        for h, (first, second) in enumerate((("x", "z"), ("z", "x")))
    )
    ga_ll = Gather(
        net, ll.at[two, eighth(8), :], ll_all,
        lambda ref, x, z: ref.at[two, x * 4 + z, eighth(8), :],
        lambda ref, x, z, h: ref.at[2 * core + h, x * 4 + z, eighth(8), :],
        "z", "x", local_sem.at[1],
    )
    ga_lm = Gather(
        net, lm_own.at[core, eighth(16), :], lm_all,
        lambda ref, x, z: ref.at[core, x * 4 + z, eighth(16), :],
        lambda ref, x, z, h: ref.at[core, x * 4 + z, pl.ds(mult(y * 16 + 8 * h, 8), 8), :],
        "x", "z", local_sem.at[2],
    )
    ga_m = Gather(
        net, m, m_all,
        lambda ref, x, z: ref.at[:, rows(x, z, 64), :],
        lambda ref, x, z, h: ref.at[h, rows(x, z, 64), :],
        "x", "z", local_sem.at[3],
    )
    ga_r = Gather(
        net, r, r_all,
        lambda ref, x, z: ref.at[:, rows(x, z, 32), :],
        lambda ref, x, z, h: ref.at[pl.ds(2 * h, 2), rows(x, z, 32), :],
        "z", "x", local_sem.at[4],
    )
    def ll_parts(o):
        return [ll_all.at[two, pl.ds(8 * g, 8), pl.ds(mult(o * 8, 8), 8), pl.ds(0, 256 * (g + 1))] for g in range(2)]

    def lm_parts(o):
        return [
            lm_all.at[core, pl.ds(4 * g, 4), pl.ds(mult(o * 16, 16), 16), pl.ds(0, 256 * (g + 1))] for g in range(4)
        ]

    ring_ll = Ring(net, ll_parts, lambda o, h: ll_parts(o)[1:] if h else ll_parts(o)[:1])
    ring_lm = Ring(net, lm_parts, lambda o, h: lm_parts(o)[:3] if h else lm_parts(o)[3:])

    mine = pl.ds(mult(net.row * 128, 128), 128)
    local_p = pltpu.make_async_copy(p.at[two], p_mine.at[:, :, mine], local_sem.at[5])
    local_p.start()
    pair_p = net.send(p.at[pl.ds(2 * other, 2)], p_mine.at[:, :, mine], "core", 1)
    small, large = (ga_ll, ga_lm), (ga_m, ga_r)
    for item in small + large:
        item.start()
    local_p.wait()
    pair_p.wait_recv()
    ring_p.start()

    base = net.col * 256

    def lower(block, first):
        at = lambda axis: lax.broadcasted_iota(jnp.int32, (256, 256), axis)
        return jnp.where(first + at(1) <= base + at(0), block, 0.0)

    for load in root_loads:
        load.wait()
    for h in range(2):
        block = lower(acc_m[h].reshape(256, 256), net.row * 512 + 256 * h)
        high[0, band(h), :256], low[0, band(h), :256] = split(jnp.transpose(block))
    left = lambda: (high[0, :512, :256], low[0, :512, :256])

    def root_terms(first, last):
        @pl.loop(first, last)
        def _(b):
            block = lower(cm[lax.div(b, 4), pl.ds(mult(lax.rem(b, 4) * 256, 256), 256), :], b * 256)
            terms[lax.div(b, 4), lax.rem(b, 4)] = dot3(left(), split(block))
            block = lower(cl[lax.div(b, 2), pl.ds(mult(lax.rem(b, 2) * 256, 256), 256), :], b * 256 + 2048)
            terms[2 + lax.div(b, 4), lax.rem(b, 4)] = dot3(left(), split(block))

    sc = TorusScatter(
        net,
        lambda o, h: terms.at[o, :, pl.ds(128 * h, 128), :],
        lambda o, h: terms.at[:, o, pl.ds(256 + 128 * h, 128), :],
        bufs_xz, bufs_zx,
    )
    ring_p.middle()
    root_terms(0, 2)
    ring_p.end()
    for item in ga_ps:
        item.start()
    for item in small:
        item.first_ring()
    root_terms(2, 4)
    for item in small:
        item.first_end()
    for item in large:
        item.first_ring()
    root_terms(4, 6)
    for a in (0, -1, 1, 2):
        for item in small:
            item.second_ring(a)
    root_terms(6, 8)
    for item in large:
        item.first_end()
    for item in small:
        for a in (0, -1, 1, 2):
            item.second_end(a)
        item.finish()
    ring_ll.start()
    ring_lm.start()
    sc.start()
    for item in ga_ps:
        item.first_ring()
    for item in large:
        item.second_ring(0)
    for item in ga_ps:
        item.first_end()
    ring_ll.middle()
    ring_lm.middle()
    for a in (-1, 1):
        for item in large:
            item.second_ring(a)
    for a in (0, -1, 1):
        for item in ga_ps:
            item.second_ring(a)
    sc.plain()
    for item in large + ga_ps:
        item.second_ring(2)
    ring_ll.end()
    ring_lm.end()
    sc.middle()
    ring_lm.finish()
    lm_loads = [pltpu.make_async_copy(lm_all.at[k], stage.at[k], load_sem.at[k]) for k in range(MIDS)]
    for load in lm_loads:
        load.start()
    for item in large + ga_ps:
        for a in (0, -1, 1, 2):
            item.second_end(a)
        item.finish()
    shared_p = []
    for o in range(4):
        part = p_all.at[two, pl.ds(128 * o, 128), :]
        shared_p.append(net.send(part, part, "core", 1))
    spread_m = Spread(net, m_all, um_c, spread_send.at[0], spread_recv.at[0], local_sem.at[6])
    spread_l = Spread(net, r_all, ul_c, spread_send.at[1], spread_recv.at[1], local_sem.at[7])
    spread_m.start()
    spread_l.start()

    def mid_nodes(lanes):
        for load in lm_loads:
            load.wait()

        @pl.loop(0, MIDS)
        def _(k):
            for j in range(4):
                total = None
                for t in range(j, 4):
                    tile = jnp.transpose(stage[k, pl.ds(4 * t, 4), :, band(j)].reshape(256, 256))
                    term = dot3(split(tile), split(m_all[k, band(t), lanes]))
                    total = term if total is None else total + term
                m_all[k, band(j), lanes] = total
                high[k, band(j), lanes], low[k, band(j), lanes] = split(total)

    ga_m.free()
    mid_nodes(pl.ds(0, 512))
    sc.turn()
    ring_ll.finish()
    for copy in shared_p:
        copy.wait_recv()
    p_loads = [
        pltpu.make_async_copy(p_all.at[i, pl.ds(64 * t, 64), :], stage.at[i // 2, i % 2 * 8 + t], load_sem.at[8 * i + t])
        for i in range(LOWS)
        for t in range(8)
    ]
    for load in p_loads:
        load.start()

    def low_nodes(first, lanes, with_g):
        for load in p_loads[8 * first : 8 * first + 16]:
            load.wait()

        @pl.loop(first, first + 2)
        def _(i):
            k = parent[i]
            own = split(lm_own[k]) if with_g else None
            for t in range(2):
                p_both = split(stage[first // 2, pl.ds((i - first) * 8 + 4 * t, 4), :, :].reshape(256, MID))
                r_all[i, band(t), lanes] -= dot3(p_both, (high[k, :, lanes], low[k, :, lanes]))
                if with_g:
                    g_in[band(t), :] = dot3_nt(p_both, own)
            for j in range(2):
                total, g_total = None, None
                for t in range(j, 2):
                    tile = split(jnp.transpose(ll_all[i, pl.ds(8 * t, 8), :, band(j)].reshape(256, 256)))
                    term = dot3(tile, split(r_all[i, band(t), lanes]))
                    total = term if total is None else total + term
                    if with_g:
                        term = dot3(tile, split(g_in[band(t), :]))
                        g_total = term if g_total is None else g_total + term
                r_all[i, band(j), lanes] = total
                if with_g:
                    g[i, band(j), :] = g_total

    both_onward = lambda first, last: (spread_m.onward(first, last), spread_l.onward(first, last))
    ga_r.free()
    low_nodes(0, pl.ds(0, 512), True)
    sc.second_middle()
    both_onward(0, 2)
    low_nodes(2, pl.ds(0, 512), True)
    both_onward(2, 4)
    for load in lm_loads:
        load.start()
    outs = lambda first: [sigma.at[pl.ds(first + 128 * h, 128), :] for h in range(2)]
    sc.end(outs(0), outs(256))
    s_high[...], s_low[...] = split(sigma[...])

    def slab(ref, unit, d, k):
        return ref.at[:, pl.ds(mult((2 * net.at("y", d) + k) * unit, unit), unit), :]

    def multiply(d, k):
        both = (slab(high, 128, d, k)[...].reshape(256, 512), slab(low, 128, d, k)[...].reshape(256, 512))
        slab(cm, 128, d, k)[...] = -dot3(both, (s_high[...], s_low[...])).reshape(MIDS, 128, 256)
        both = split(slab(r_all, 64, d, k)[...].reshape(256, 512))
        slab(cl, 64, d, k)[...] = -dot3(both, (s_high[...], s_low[...])).reshape(LOWS, 64, 256)

    order = (2, 1, -1, 0)
    pairs = {}
    for d in order:
        multiply(d, other)
        pairs[d] = [
            net.send(slab(cm, 128, d, other), core_m.at[d % 4], "core", 1),
            net.send(slab(cl, 64, d, other), core_l.at[d % 4], "core", 1),
        ]
    firsts = []
    for d in order:
        if d == -1:
            both_onward(4, CHUNKS + 2)
        multiply(d, core)
        for copy in pairs[d]:
            copy.wait_recv()
        acc_m[d % 4] = core_m[d % 4] + slab(cm, 128, d, core)[...]
        acc_l[d % 4] = core_l[d % 4] + slab(cl, 64, d, core)[...]
        if d == 2:
            firsts = [net.send(acc_m.at[2], near_m, "y", 1), net.send(acc_l.at[2], near_l, "y", -1)]
    seconds = [net.send(acc_l.at[1], far_l.at[0], "y", 1), net.send(acc_m.at[3], far_m.at[1], "y", -1)]

    block_column = pl.ds(0, 256)
    spread_m.finish()
    spread_l.finish()
    column_loads = [
        pltpu.make_async_copy(src, dst.at[:, :, block_column], local_sem.at[index])
        for index, (src, dst) in enumerate(((um_c, m_all), (ul_c, r_all)))
    ]
    for load in column_loads:
        load.start()
    for load in column_loads:
        load.wait()
    mid_nodes(block_column)
    for load in p_loads:
        load.start()
    column_out = [
        pltpu.make_async_copy(src.at[:, :, block_column], dst, local_sem.at[index])
        for index, (dst, src) in enumerate(((um_c, m_all), (ul_c, r_all)))
    ]
    column_out[0].start()
    firsts[0].wait_recv()
    near_m[...] += acc_m[1]
    seconds.append(net.send(near_m, far_m.at[0], "y", 1))
    firsts[1].wait_recv()
    near_l[...] += acc_l[3]
    seconds.append(net.send(near_l, far_l.at[1], "y", -1))
    low_nodes(0, block_column, False)
    low_nodes(2, block_column, False)
    column_out[1].start()
    for copy in seconds:
        copy.wait_recv()
    out_m[...] = acc_m[0] + far_m[0] + far_m[1]
    out_l[...] = acc_l[0] + far_l[0] + far_l[1]
    for copy in column_out:
        copy.wait()
    net.finish()


SEMS = 240


def main_step(*arrays):
    shape = lambda *dims: jax.ShapeDtypeStruct(dims, F32)
    vmem, hbm = pl.BlockSpec(memory_space=VMEM), pl.BlockSpec(memory_space=ANY)
    block = lambda *dims: VMEM(dims, F32)
    half = lambda *dims: VMEM(dims, jnp.bfloat16)
    return pl.pallas_call(
        main_kernel,
        out_shape=(
            shape(512, 256), shape(MIDS, 128, 256), shape(LOWS, 64, 256), shape(LOWS, LOW, 64),
            shape(MIDS, MID, 256), shape(LOWS, LOW, 256), shape(MIDS, 16, 64, MID), shape(LOWS, LOW, MID),
        ),
        in_specs=[pl.BlockSpec(memory_space=pltpu.SMEM), hbm, vmem] + [hbm] * 4,
        out_specs=[vmem] * 4 + [hbm] * 4,
        scratch_shapes=[
            block(MIDS, MID, 512), block(LOWS, LOW, 512), block(2, 32, MID), block(LOW, 64),
            block(LOWS, 16, 32, LOW), block(MIDS, 16, 64, MID), half(MIDS, MID, 512), half(MIDS, MID, 512),
            half(512, 256), half(512, 256), block(4, 4, 512, 256), block(MIDS, MID, 256), block(LOWS, LOW, 256),
            block(4, MIDS, 128, 256), block(4, LOWS, 64, 256), block(4, MIDS, 128, 256), block(4, LOWS, 64, 256),
            block(MIDS, 128, 256), block(LOWS, 64, 256), block(2, MIDS, 128, 256), block(2, LOWS, 64, 256),
        ] + torus_bufs(128, 256) + torus_bufs(128, 256) + [
            pltpu.SemaphoreType.DMA((SEMS,)),
            pltpu.SemaphoreType.DMA((SEMS,)),
            pltpu.SemaphoreType.DMA((2, 4 * CHUNKS)),
            pltpu.SemaphoreType.DMA((2, 4 * CHUNKS)),
            pltpu.SemaphoreType.DMA((8,)),
            pltpu.SemaphoreType.DMA((32,)),
        ],
        compiler_params=params(0),
        name="main_step",
    )(*arrays)


DIAG_ROWS = 320


def third_kernel(parent, mid_cross, low_root, um, ul, g, lm, ll, out, terms, lm_t, ll_t, *scratch):
    bufs_xz, bufs_zx, (send_sem, recv_sem) = scratch[:5], scratch[5:10], scratch[10:]
    net = Net(send_sem, recv_sem)
    net.greet(("x", "z"))
    for p in range(MIDS):
        lm_t[p] = jnp.transpose(lm[p])
    for i in range(LOWS):
        ll_t[i] = jnp.transpose(ll[i])
    low_rows = pl.ds(mult(net.row * 64, 64), 64)
    for p in range(MIDS):
        mine = split(lm_t[p, pl.ds(mult(net.row * 128, 128), 128), :])
        term = dot3_nt(split(lm_t[p]), mine) - dot3_nt(split(um[p]), split(mid_cross[p]))
        terms[:, :, pl.ds(64 * p, 64), :] = term.reshape(4, 4, 64, 128)
    for pair in range(2):
        par, own = [], []
        for i in (2 * pair, 2 * pair + 1):
            p = parent[i]
            root, g_mine = split(low_root[i]), split(g[i, low_rows, :])
            par.append(-(dot3_nt(split(um[p]), root) + dot3_nt(split(lm_t[p]), g_mine)))
            own.append(
                dot3_nt(split(ll_t[i]), split(ll_t[i, low_rows, :])) + dot3_nt(split(g[i]), g_mine)
                - dot3_nt(split(ul[i]), root)
            )
        terms[:, :, pl.ds(128 + 64 * pair, 64), :] = jnp.concatenate(par, axis=1).reshape(4, 4, 64, 128)
        terms[:, :, pl.ds(256 + 32 * pair, 32), :] = jnp.concatenate(own, axis=1).reshape(4, 4, 32, 128)
    half = DIAG_ROWS // 4

    def outs(base):
        return [out.at[pl.ds(base + half * h, half), :] for h in range(2)]

    sc = TorusScatter(
        net,
        lambda o, h: terms.at[o, :, pl.ds(half * h, half), :],
        lambda o, h: terms.at[:, o, pl.ds(2 * half + half * h, half), :],
        bufs_xz, bufs_zx,
    )
    sc.start()
    sc.plain()
    sc.middle()
    sc.turn()
    sc.second_middle()
    sc.end(outs(0), outs(2 * half))
    net.finish()


def third_step(parent, *arrays):
    return pl.pallas_call(
        third_kernel,
        out_shape=jax.ShapeDtypeStruct((DIAG_ROWS, 128), F32),
        in_specs=[pl.BlockSpec(memory_space=pltpu.SMEM)] + [pl.BlockSpec(memory_space=VMEM)] * 7,
        out_specs=pl.BlockSpec(memory_space=VMEM),
        scratch_shapes=[
            VMEM((4, 4, DIAG_ROWS, 128), F32), VMEM((MIDS, MID, 64), F32), VMEM((LOWS, LOW, 32), F32),
        ] + torus_bufs(DIAG_ROWS // 4, 128) + torus_bufs(DIAG_ROWS // 4, 128) + [
            pltpu.SemaphoreType.DMA((32,)),
            pltpu.SemaphoreType.DMA((32,)),
        ],
        compiler_params=params(1),
        name="third_step",
    )(parent, *arrays)


def lower_part(factor):
    rows_here = factor.shape[1]
    row_ids = lax.axis_index("col") * rows_here + lax.broadcasted_iota(jnp.int32, factor.shape[1:], 0)
    col_ids = lax.broadcasted_iota(jnp.int32, factor.shape[1:], 1)
    return jnp.where((col_ids <= row_ids)[None], factor, 0.0)


def live_mask(local_rows, first_row, structure, block_shift):
    row_ids = first_row + jnp.arange(local_rows, dtype=jnp.int32)
    block_ids = row_ids // BLOCK + block_shift
    return jnp.any(block_ids[None, :, None] == structure[:, None, :], axis=2).astype(F32)


def local(root_factor, mid_factor, low_factor, mid_rows, low_parent_rows, low_root_rows, mid_struct, low_struct, low_parent):
    row = lax.axis_index("row")
    lm = lower_part(mid_factor)
    ll = lower_part(low_factor)
    m = jnp.transpose(mid_rows, (0, 2, 1)) * live_mask(512, row * 512, mid_struct, 0)[:, None, :]
    r = jnp.transpose(low_root_rows, (0, 2, 1)) * live_mask(512, row * 512, low_struct, MID // BLOCK)[:, None, :]
    p = jnp.transpose(low_parent_rows, (0, 2, 1)) * live_mask(128, row * 128, low_struct, 0)[:, None, :]
    sigma, mid_cross, low_root, g, um_c, ul_c, _, _ = main_step(low_parent, root_factor, lm, m, r, p, ll)
    sums = third_step(low_parent, mid_cross, low_root, um_c, ul_c, g, lm, ll)
    mid_diag = jnp.transpose(sums[:128].reshape(2, 64, 128), (0, 2, 1))
    par = sums[128:256].reshape(2, 64, 2, 64)
    low_cross_parent = jnp.transpose(par, (0, 2, 3, 1)).reshape(4, 64, 64)
    low = sums[256:].reshape(2, 32, 2, 64)
    low_diag = jnp.transpose(low, (0, 2, 3, 1)).reshape(4, 64, 32)
    return sigma, mid_diag, mid_cross, low_diag, low_cross_parent, low_root


def solution(mesh):
    rc = P(None, "row", "col")
    in_specs = (P("col", None), P(None, "col", None), P(None, "col", None), rc, rc, rc, P(), P(), P())
    out_specs = (P("row", "col"), rc, rc, rc, rc, rc)
    return jax.shard_map(local, mesh=mesh, in_specs=in_specs, out_specs=out_specs, check_vma=False)
```

```python
import functools

import jax
import jax.numpy as jnp
from jax import lax
from jax.experimental import pallas as pl
from jax.experimental.pallas import tpu as pltpu
from jax.sharding import PartitionSpec as P

BLOCK = 256
ROOT = 4096
MID = 1024
LOW = 512
MIDS = 2
LOWS = 4
MESH = pl.DeviceIdType.MESH
F32 = jnp.float32
VMEM = pltpu.VMEM
ANY = pl.ANY


class Net:
    def __init__(self, send_sem, recv_sem):
        self.row = lax.axis_index("row")
        self.col = lax.axis_index("col")
        self.place = {
            "x": lax.div(self.col, 4),
            "z": lax.rem(self.col, 4),
            "y": lax.div(self.row, 2),
            "core": lax.rem(self.row, 2),
        }
        self.send_sem, self.recv_sem, self.used, self.started = send_sem, recv_sem, 0, []

    def at(self, axis, shift):
        if axis == "core":
            return lax.rem(self.place["core"] + shift, 2)
        return lax.rem(self.place[axis] + shift + 4, 4)

    def device(self, **shifts):
        at = {axis: self.at(axis, shifts.get(axis, 0)) for axis in self.place}
        return (at["y"] * 2 + at["core"], at["x"] * 4 + at["z"])

    def greet(self, axes):
        barrier = pltpu.get_barrier_semaphore()
        count = 0
        for axis in axes:
            for shift in (1,) if axis == "core" else (1, -1):
                pl.semaphore_signal(barrier, inc=1, device_id=self.device(**{axis: shift}), device_id_type=MESH)
                count += 1
        pl.semaphore_wait(barrier, count)

    def send(self, src, dst, axis, shift):
        index = self.used
        self.used += 1
        copy = pltpu.make_async_remote_copy(
            src_ref=src,
            dst_ref=dst,
            send_sem=self.send_sem.at[index],
            recv_sem=self.recv_sem.at[index],
            device_id=self.device(**{axis: shift}),
            device_id_type=MESH,
        )
        copy.start()
        self.started.append(copy)
        return copy

    def finish(self):
        for copy in self.started:
            copy.wait_send()


def mult(value, unit):
    return pl.multiple_of(value, unit)


def params(collective_id):
    return pltpu.CompilerParams(collective_id=collective_id, has_side_effects=True, vmem_limit_bytes=62 * 2**20)


class Gather:
    def __init__(self, net, src, dst, whole, half, first, second, local_sem, share=None):
        self.net, self.dst, self.whole, self.half = net, dst, whole, half
        self.first, self.second, self.share = first, second, share
        self.src, self.local_sem, self.sent = src, local_sem, []

    def send(self, *args):
        copy = self.net.send(*args)
        self.sent.append(copy)
        return copy

    def free(self):
        for copy in self.sent:
            copy.wait_send()
        self.net.started = [copy for copy in self.net.started if not any(copy is one for one in self.sent)]

    def spot(self, a, b):
        at = {self.first: self.net.at(self.first, a), self.second: self.net.at(self.second, b)}
        return at["x"], at["z"]

    def piece(self, a, b):
        return self.whole(self.dst, *self.spot(a, b))

    def part(self, a, b, h):
        return self.half(self.dst, *self.spot(a, b), h)

    def start(self):
        net, own = self.net, self.piece(0, 0)
        self.local = pltpu.make_async_copy(self.src, own, self.local_sem)
        self.local.start()
        self.p1 = [self.send(self.src, own, self.first, s) for s in (1, -1)]
        self.p2 = {0: [self.send(self.src, own, self.second, s) for s in (1, -1)]}

    def onward(self, a):
        piece = self.piece(a, 0)
        self.p2[a] = [self.send(piece, piece, self.second, s) for s in (1, -1)]

    def first_ring(self):
        self.fwd = []
        for index, shift in enumerate((1, -1)):
            self.p1[index].wait_recv()
            part = self.part(-shift, 0, index)
            self.fwd.append(self.send(part, part, self.first, shift))
            self.onward(-shift)

    def first_end(self):
        for copy in self.fwd:
            copy.wait_recv()
        self.onward(2)

    def second_ring(self, a):
        copies = []
        for index, shift in enumerate((1, -1)):
            self.p2[a][index].wait_recv()
            part = self.part(a, -shift, index)
            copies.append(self.send(part, part, self.second, shift))
        self.p2[a] = copies

    def second_end(self, a):
        for copy in self.p2[a]:
            copy.wait_recv()

    def finish(self):
        self.local.wait()


class Scatter:
    def __init__(self, net, axis, part, near, far):
        self.net, self.axis, self.part, self.near, self.far = net, axis, part, near, far

    def start(self):
        opposite = self.net.at(self.axis, 2)
        self.first = [
            self.net.send(self.part(opposite, h), self.near[h], self.axis, shift) for h, shift in enumerate((1, -1))
        ]

    def plain(self):
        self.second = [
            self.net.send(self.part(self.net.at(self.axis, shift), 1 - h), self.far[h][1 - h], self.axis, shift)
            for h, shift in enumerate((1, -1))
        ]

    def middle(self):
        for h, shift in enumerate((1, -1)):
            self.first[h].wait_recv()
            self.near[h][...] += self.part(self.net.at(self.axis, shift), h)[...]
            self.second.append(self.net.send(self.near[h], self.far[h][h], self.axis, shift))

    def end(self, out):
        for copy in self.second:
            copy.wait_recv()
        for h in range(2):
            out[h][...] = self.part(self.net.at(self.axis, 0), h)[...] + self.far[0][h][...] + self.far[1][h][...]


class TorusScatter:
    def __init__(self, net, part_xz, part_zx, bufs_xz, bufs_zx):
        self.net, self.bufs = net, (bufs_xz, bufs_zx)
        self.stages = [self.stage(axis, part, bufs[0], bufs[1])
                       for axis, part, bufs in (("x", part_xz, bufs_xz), ("z", part_zx, bufs_zx))]

    def stage(self, axis, part, near, far):
        return Scatter(self.net, axis, part, [near.at[0], near.at[1]], [[far.at[s, h] for h in range(2)] for s in range(2)])

    def start(self):
        for stage in self.stages:
            stage.start()

    def plain(self):
        for stage in self.stages:
            stage.plain()

    def middle(self):
        for stage in self.stages:
            stage.middle()

    def turn(self):
        later = []
        for stage, axis, bufs in zip(self.stages, ("z", "x"), self.bufs):
            sums = bufs[2]
            stage.end([sums.at[0], sums.at[1]])
            part = functools.partial(lambda sums, o, h: sums.at[h, o], sums)
            later.append(self.stage(axis, part, bufs[3], bufs[4]))
            later[-1].start()
            later[-1].plain()
        self.stages = later

    second_middle = middle

    def end(self, out_xz, out_zx):
        for stage, out in zip(self.stages, (out_xz, out_zx)):
            stage.end(out)


def torus_bufs(rows, lanes):
    return [
        VMEM((2, 4, rows, lanes), F32),
        VMEM((2, 2, 4, rows, lanes), F32),
        VMEM((2, 4, rows, lanes), F32),
        VMEM((2, rows, lanes), F32),
        VMEM((2, 2, rows, lanes), F32),
    ]


def split(a):
    high = a.astype(jnp.bfloat16)
    return high, (a - high.astype(F32)).astype(jnp.bfloat16)


def dot3(a, b):
    go = functools.partial(jnp.dot, preferred_element_type=F32)
    return go(a[0], b[0]) + (go(a[0], b[1]) + go(a[1], b[0]))


class Ring:
    def __init__(self, net, pieces, halves, share=True):
        self.net, self.pieces, self.halves, self.share = net, pieces, halves, share

    def pair_up(self, place):
        if self.share:
            self.pair += [self.net.send(part, part, "core", 1) for part in self.pieces(place)]

    def start(self):
        own = self.pieces(self.net.at("y", 0))
        self.near = [[self.net.send(part, part, "y", s) for part in own] for s in (1, -1)]
        self.pair = []
        self.pair_up(self.net.at("y", 0))

    def middle(self):
        self.far = []
        for index, shift in enumerate((1, -1)):
            for copy in self.near[index]:
                copy.wait_recv()
            place = self.net.at("y", -shift)
            self.far += [self.net.send(part, part, "y", shift) for part in self.halves(place, index)]
            self.pair_up(place)

    def end(self):
        for copy in self.far:
            copy.wait_recv()
        self.pair_up(self.net.at("y", 2))

    def finish(self):
        for copy in self.pair:
            copy.wait_recv()


CHUNKS = 4
STEP = 256


class Spread:
    def __init__(self, net, source, out, send_sem, recv_sem, local_sem):
        self.net, self.source, self.out = net, source, out
        self.send_sem, self.recv_sem, self.local_sem = send_sem, recv_sem, local_sem
        x, z = net.place["x"], net.place["z"]
        self.lanes = pl.ds(mult(lax.rem(z, 2) * 256, 256), 256)
        self.away = lax.rem(net.place["y"] - x + 4, 4)
        self.is_core = net.place["core"] == lax.div(z, 2)

    def spot(self, ref, way, chunk, lanes):
        per = ref.shape[1] // STEP
        return ref.at[way * (ref.shape[0] // 2) + chunk // per, pl.ds(chunk % per * STEP, STEP), lanes]

    def copy(self, way, chunk, pair):
        place = self.spot(self.out, way, chunk, slice(None))
        index = pair * 2 * CHUNKS + way * CHUNKS + chunk
        to = {"core": 1} if pair else {"y": 1 - 2 * way}
        return pltpu.make_async_remote_copy(
            src_ref=place, dst_ref=place,
            send_sem=self.send_sem.at[index], recv_sem=self.recv_sem.at[index],
            device_id=self.net.device(**to), device_id_type=MESH,
        )

    def load(self):
        return pltpu.make_async_copy(self.source.at[:, :, self.lanes], self.out, self.local_sem)

    def start(self):
        @pl.when(jnp.logical_and(self.is_core, self.away == 0))
        def _():
            self.load().start()
            self.load().wait()
            for pair in range(2):
                for chunk in range(CHUNKS):
                    for way in range(2):
                        self.copy(way, chunk, pair).start()

    def onward(self, first, last):
        for away in (1, 2, 3):
            @pl.when(jnp.logical_and(self.is_core, self.away == away))
            def _():
                for step in range(first, last):
                    for way in range(2):
                        hops = away if way == 0 else 4 - away
                        chunk = step + 1 - hops
                        if 0 <= chunk < CHUNKS:
                            self.copy(way, chunk, 0).wait_recv()
                            if hops < 3:
                                self.copy(way, chunk, 0).start()
                            self.copy(way, chunk, 1).start()

    def finish(self):
        for chunk in range(CHUNKS):
            for way in range(2):
                @pl.when(jnp.logical_and(self.is_core, self.away != (3, 1)[way]))
                def _():
                    self.copy(way, chunk, 0).wait_send()

                @pl.when(self.is_core)
                def _():
                    self.copy(way, chunk, 1).wait_send()

                @pl.when(jnp.logical_not(self.is_core))
                def _():
                    self.copy(way, chunk, 1).wait_recv()


def dot3_nt(a, b):
    go = lambda s, t: lax.dot_general(s, t, (((1,), (1,)), ((), ())), preferred_element_type=F32)
    return go(a[0], b[0]) + (go(a[0], b[1]) + go(a[1], b[0]))


def main_kernel(parent, lr, lm_own, m, r, p, ll, sigma, out_m, out_l, g, um_c, ul_c, lm_all, p_all,
                m_all, r_all, p_mine, g_in, ll_all, stage, high, low, s_high, s_low, terms, cm, cl,
                acc_m, acc_l, core_m, core_l, near_m, near_l, far_m, far_l, *scratch):
    bufs_xz, bufs_zx, (send_sem, recv_sem, spread_send, spread_recv, local_sem, load_sem) = (
        scratch[:5], scratch[5:10], scratch[10:]
    )
    net = Net(send_sem, recv_sem)
    core, y = net.place["core"], net.place["y"]
    other = 1 - core

    def band(block):
        return pl.ds(block * 256, 256)

    def root_block(b):
        return cm.at[b // 4, band(b % 4), :] if b < 8 else cl.at[(b - 8) // 2, band(b % 2), :]

    root_loads = [
        pltpu.make_async_copy(
            lr.at[pl.ds(128 * t, 128), pl.ds(mult(net.row * 512 + 256 * h, 256), 256)], acc_m.at[h, t], load_sem.at[2 * h + t]
        )
        for h in range(2)
        for t in range(2)
    ]
    root_loads += [pltpu.make_async_copy(lr.at[:, band(b)], root_block(b), load_sem.at[4 + b]) for b in range(16)]
    for load in root_loads:
        load.start()
    net.greet(("x", "z", "y", "core"))

    def rows(x, z, n):
        return pl.ds(mult((x * 4 + z) * n, n), n)

    def eighth(n):
        return pl.ds(mult(y * n, n), n)

    two = pl.ds(2 * core, 2)
    def p_lanes(o):
        return pl.ds(mult(o * 256, 256), 256)

    ring_p = Ring(net, lambda o: [p_mine.at[:, :, p_lanes(o)]], lambda o, h: [p_mine.at[h, :, p_lanes(o)]], share=False)
    ga_ps = tuple(
        Gather(
            net, p_mine.at[h], p_all,
            lambda ref, x, z, h=h: ref.at[2 * core + h, rows(x, z, 32), :],
            lambda ref, x, z, part, h=h: ref.at[2 * core + h, pl.ds(mult((x * 4 + z) * 32 + 16 * part, 16), 16), :],
            first, second, local_sem.at[(0, 5)[h]],
        )
        for h, (first, second) in enumerate((("x", "z"), ("z", "x")))
    )
    ga_ll = Gather(
        net, ll.at[two, eighth(8), :], ll_all,
        lambda ref, x, z: ref.at[two, x * 4 + z, eighth(8), :],
        lambda ref, x, z, h: ref.at[2 * core + h, x * 4 + z, eighth(8), :],
        "z", "x", local_sem.at[1],
    )
    ga_lm = Gather(
        net, lm_own.at[core, eighth(16), :], lm_all,
        lambda ref, x, z: ref.at[core, x * 4 + z, eighth(16), :],
        lambda ref, x, z, h: ref.at[core, x * 4 + z, pl.ds(mult(y * 16 + 8 * h, 8), 8), :],
        "x", "z", local_sem.at[2],
    )
    ga_m = Gather(
        net, m, m_all,
        lambda ref, x, z: ref.at[:, rows(x, z, 64), :],
        lambda ref, x, z, h: ref.at[h, rows(x, z, 64), :],
        "x", "z", local_sem.at[3],
    )
    ga_r = Gather(
        net, r, r_all,
        lambda ref, x, z: ref.at[:, rows(x, z, 32), :],
        lambda ref, x, z, h: ref.at[pl.ds(2 * h, 2), rows(x, z, 32), :],
        "z", "x", local_sem.at[4],
    )
    def ll_parts(o):
        return [ll_all.at[two, pl.ds(8 * g, 8), pl.ds(mult(o * 8, 8), 8), pl.ds(0, 256 * (g + 1))] for g in range(2)]

    def lm_parts(o):
        return [
            lm_all.at[core, pl.ds(4 * g, 4), pl.ds(mult(o * 16, 16), 16), pl.ds(0, 256 * (g + 1))] for g in range(4)
        ]

    ring_ll = Ring(net, ll_parts, lambda o, h: ll_parts(o)[1:] if h else ll_parts(o)[:1])
    ring_lm = Ring(net, lm_parts, lambda o, h: lm_parts(o)[:3] if h else lm_parts(o)[3:])

    mine = pl.ds(mult(net.row * 128, 128), 128)
    local_p = pltpu.make_async_copy(p.at[two], p_mine.at[:, :, mine], local_sem.at[5])
    local_p.start()
    pair_p = net.send(p.at[pl.ds(2 * other, 2)], p_mine.at[:, :, mine], "core", 1)
    small, large = (ga_ll, ga_lm), (ga_m, ga_r)
    for item in small + large:
        item.start()
    local_p.wait()
    pair_p.wait_recv()
    ring_p.start()

    base = net.col * 256

    def lower(block, first):
        at = lambda axis: lax.broadcasted_iota(jnp.int32, (256, 256), axis)
        return jnp.where(first + at(1) <= base + at(0), block, 0.0)

    for load in root_loads:
        load.wait()
    for h in range(2):
        block = lower(acc_m[h].reshape(256, 256), net.row * 512 + 256 * h)
        high[0, band(h), :256], low[0, band(h), :256] = split(jnp.transpose(block))
    left = lambda: (high[0, :512, :256], low[0, :512, :256])

    def root_terms(first, last):
        @pl.loop(first, last)
        def _(b):
            block = lower(cm[lax.div(b, 4), pl.ds(mult(lax.rem(b, 4) * 256, 256), 256), :], b * 256)
            terms[lax.div(b, 4), lax.rem(b, 4)] = dot3(left(), split(block))
            block = lower(cl[lax.div(b, 2), pl.ds(mult(lax.rem(b, 2) * 256, 256), 256), :], b * 256 + 2048)
            terms[2 + lax.div(b, 4), lax.rem(b, 4)] = dot3(left(), split(block))

    sc = TorusScatter(
        net,
        lambda o, h: terms.at[o, :, pl.ds(128 * h, 128), :],
        lambda o, h: terms.at[:, o, pl.ds(256 + 128 * h, 128), :],
        bufs_xz, bufs_zx,
    )
    ring_p.middle()
    root_terms(0, 2)
    ring_p.end()
    for item in ga_ps:
        item.start()
    for item in small:
        item.first_ring()
    root_terms(2, 4)
    for item in small:
        item.first_end()
    for item in large:
        item.first_ring()
    root_terms(4, 6)
    for a in (0, -1, 1, 2):
        for item in small:
            item.second_ring(a)
    root_terms(6, 8)
    for item in large:
        item.first_end()
    for item in small:
        for a in (0, -1, 1, 2):
            item.second_end(a)
        item.finish()
    ring_ll.start()
    ring_lm.start()
    for item in ga_ps:
        item.first_ring()
    for item in large:
        item.second_ring(0)
    for item in ga_ps:
        item.first_end()
    ring_ll.middle()
    ring_lm.middle()
    for a in (-1, 1):
        for item in large:
            item.second_ring(a)
    for a in (0, -1, 1):
        for item in ga_ps:
            item.second_ring(a)
    for item in large + ga_ps:
        item.second_ring(2)
    sc.start()
    sc.plain()
    ring_ll.end()
    ring_lm.end()
    ring_lm.finish()
    lm_loads = [pltpu.make_async_copy(lm_all.at[k], stage.at[k], load_sem.at[k]) for k in range(MIDS)]
    for load in lm_loads:
        load.start()
    for item in large + ga_ps:
        for a in (0, -1, 1, 2):
            item.second_end(a)
        item.finish()
    shared_p = []
    for o in range(4):
        part = p_all.at[two, pl.ds(128 * o, 128), :]
        shared_p.append(net.send(part, part, "core", 1))
    spread_m = Spread(net, m_all, um_c, spread_send.at[0], spread_recv.at[0], local_sem.at[6])
    spread_l = Spread(net, r_all, ul_c, spread_send.at[1], spread_recv.at[1], local_sem.at[7])
    spread_m.start()
    spread_l.start()

    def mid_nodes(lanes):
        for load in lm_loads:
            load.wait()

        @pl.loop(0, MIDS)
        def _(k):
            for j in range(4):
                total = None
                for t in range(j, 4):
                    tile = jnp.transpose(stage[k, pl.ds(4 * t, 4), :, band(j)].reshape(256, 256))
                    term = dot3(split(tile), split(m_all[k, band(t), lanes]))
                    total = term if total is None else total + term
                m_all[k, band(j), lanes] = total
                high[k, band(j), lanes], low[k, band(j), lanes] = split(total)

    ga_m.free()
    mid_nodes(pl.ds(0, 512))
    sc.middle()
    ring_ll.finish()
    for copy in shared_p:
        copy.wait_recv()
    p_loads = [
        pltpu.make_async_copy(p_all.at[i, pl.ds(64 * t, 64), :], stage.at[i // 2, i % 2 * 8 + t], load_sem.at[8 * i + t])
        for i in range(LOWS)
        for t in range(8)
    ]
    for load in p_loads:
        load.start()

    def low_nodes(first, lanes, with_g):
        for load in p_loads[8 * first : 8 * first + 16]:
            load.wait()

        @pl.loop(first, first + 2)
        def _(i):
            k = parent[i]
            own = split(lm_own[k]) if with_g else None
            for t in range(2):
                p_both = split(stage[first // 2, pl.ds((i - first) * 8 + 4 * t, 4), :, :].reshape(256, MID))
                r_all[i, band(t), lanes] -= dot3(p_both, (high[k, :, lanes], low[k, :, lanes]))
                if with_g:
                    g_in[band(t), :] = dot3_nt(p_both, own)
            for j in range(2):
                total, g_total = None, None
                for t in range(j, 2):
                    tile = split(jnp.transpose(ll_all[i, pl.ds(8 * t, 8), :, band(j)].reshape(256, 256)))
                    term = dot3(tile, split(r_all[i, band(t), lanes]))
                    total = term if total is None else total + term
                    if with_g:
                        term = dot3(tile, split(g_in[band(t), :]))
                        g_total = term if g_total is None else g_total + term
                r_all[i, band(j), lanes] = total
                if with_g:
                    g[i, band(j), :] = g_total

    both_onward = lambda first, last: (spread_m.onward(first, last), spread_l.onward(first, last))
    ga_r.free()
    both_onward(0, 1)
    low_nodes(0, pl.ds(0, 512), True)
    sc.turn()
    both_onward(1, 3)
    sc.second_middle()
    low_nodes(2, pl.ds(0, 512), True)
    both_onward(3, 5)
    for load in lm_loads:
        load.start()
    outs = lambda first: [sigma.at[pl.ds(first + 128 * h, 128), :] for h in range(2)]
    sc.end(outs(0), outs(256))
    s_high[...], s_low[...] = split(sigma[...])

    def slab(ref, unit, d, k):
        return ref.at[:, pl.ds(mult((2 * net.at("y", d) + k) * unit, unit), unit), :]

    def multiply(d, k):
        both = (slab(high, 128, d, k)[...].reshape(256, 512), slab(low, 128, d, k)[...].reshape(256, 512))
        slab(cm, 128, d, k)[...] = -dot3(both, (s_high[...], s_low[...])).reshape(MIDS, 128, 256)
        both = split(slab(r_all, 64, d, k)[...].reshape(256, 512))
        slab(cl, 64, d, k)[...] = -dot3(both, (s_high[...], s_low[...])).reshape(LOWS, 64, 256)

    order = (2, 1, -1, 0)
    pairs = {}
    for d in order:
        multiply(d, other)
        pairs[d] = [
            net.send(slab(cm, 128, d, other), core_m.at[d % 4], "core", 1),
            net.send(slab(cl, 64, d, other), core_l.at[d % 4], "core", 1),
        ]
    firsts = []
    for d in order:
        if d == -1:
            both_onward(5, CHUNKS + 2)
        multiply(d, core)
        for copy in pairs[d]:
            copy.wait_recv()
        acc_m[d % 4] = core_m[d % 4] + slab(cm, 128, d, core)[...]
        acc_l[d % 4] = core_l[d % 4] + slab(cl, 64, d, core)[...]
        if d == 2:
            firsts = [net.send(acc_m.at[2], near_m, "y", 1), net.send(acc_l.at[2], near_l, "y", -1)]
    seconds = [net.send(acc_l.at[1], far_l.at[0], "y", 1), net.send(acc_m.at[3], far_m.at[1], "y", -1)]

    block_column = pl.ds(0, 256)
    spread_m.finish()
    spread_l.finish()
    column_loads = [
        pltpu.make_async_copy(src, dst.at[:, :, block_column], local_sem.at[index])
        for index, (src, dst) in enumerate(((um_c, m_all), (ul_c, r_all)))
    ]
    for load in column_loads:
        load.start()
    for load in column_loads:
        load.wait()
    mid_nodes(block_column)
    for load in p_loads:
        load.start()
    column_out = [
        pltpu.make_async_copy(src.at[:, :, block_column], dst, local_sem.at[index])
        for index, (dst, src) in enumerate(((um_c, m_all), (ul_c, r_all)))
    ]
    column_out[0].start()
    firsts[0].wait_recv()
    near_m[...] += acc_m[1]
    seconds.append(net.send(near_m, far_m.at[0], "y", 1))
    firsts[1].wait_recv()
    near_l[...] += acc_l[3]
    seconds.append(net.send(near_l, far_l.at[1], "y", -1))
    low_nodes(0, block_column, False)
    low_nodes(2, block_column, False)
    column_out[1].start()
    for copy in seconds:
        copy.wait_recv()
    out_m[...] = acc_m[0] + far_m[0] + far_m[1]
    out_l[...] = acc_l[0] + far_l[0] + far_l[1]
    for copy in column_out:
        copy.wait()
    net.finish()


SEMS = 240


def main_step(*arrays):
    shape = lambda *dims: jax.ShapeDtypeStruct(dims, F32)
    vmem, hbm = pl.BlockSpec(memory_space=VMEM), pl.BlockSpec(memory_space=ANY)
    block = lambda *dims: VMEM(dims, F32)
    half = lambda *dims: VMEM(dims, jnp.bfloat16)
    return pl.pallas_call(
        main_kernel,
        out_shape=(
            shape(512, 256), shape(MIDS, 128, 256), shape(LOWS, 64, 256), shape(LOWS, LOW, 64),
            shape(MIDS, MID, 256), shape(LOWS, LOW, 256), shape(MIDS, 16, 64, MID), shape(LOWS, LOW, MID),
        ),
        in_specs=[pl.BlockSpec(memory_space=pltpu.SMEM), hbm, vmem] + [hbm] * 4,
        out_specs=[vmem] * 4 + [hbm] * 4,
        scratch_shapes=[
            block(MIDS, MID, 512), block(LOWS, LOW, 512), block(2, 32, MID), block(LOW, 64),
            block(LOWS, 16, 32, LOW), block(MIDS, 16, 64, MID), half(MIDS, MID, 512), half(MIDS, MID, 512),
            half(512, 256), half(512, 256), block(4, 4, 512, 256), block(MIDS, MID, 256), block(LOWS, LOW, 256),
            block(4, MIDS, 128, 256), block(4, LOWS, 64, 256), block(4, MIDS, 128, 256), block(4, LOWS, 64, 256),
            block(MIDS, 128, 256), block(LOWS, 64, 256), block(2, MIDS, 128, 256), block(2, LOWS, 64, 256),
        ] + torus_bufs(128, 256) + torus_bufs(128, 256) + [
            pltpu.SemaphoreType.DMA((SEMS,)),
            pltpu.SemaphoreType.DMA((SEMS,)),
            pltpu.SemaphoreType.DMA((2, 4 * CHUNKS)),
            pltpu.SemaphoreType.DMA((2, 4 * CHUNKS)),
            pltpu.SemaphoreType.DMA((8,)),
            pltpu.SemaphoreType.DMA((32,)),
        ],
        compiler_params=params(0),
        name="main_step",
    )(*arrays)


DIAG_ROWS = 320


def third_kernel(parent, mid_cross, low_root, um, ul, g, lm, ll, out, terms, lm_t, ll_t, *scratch):
    bufs_xz, bufs_zx, (send_sem, recv_sem) = scratch[:5], scratch[5:10], scratch[10:]
    net = Net(send_sem, recv_sem)
    net.greet(("x", "z"))
    for p in range(MIDS):
        lm_t[p] = jnp.transpose(lm[p])
    for i in range(LOWS):
        ll_t[i] = jnp.transpose(ll[i])
    low_rows = pl.ds(mult(net.row * 64, 64), 64)
    for p in range(MIDS):
        mine = split(lm_t[p, pl.ds(mult(net.row * 128, 128), 128), :])
        term = dot3_nt(split(lm_t[p]), mine) - dot3_nt(split(um[p]), split(mid_cross[p]))
        terms[:, :, pl.ds(64 * p, 64), :] = term.reshape(4, 4, 64, 128)
    for pair in range(2):
        par, own = [], []
        for i in (2 * pair, 2 * pair + 1):
            p = parent[i]
            root, g_mine = split(low_root[i]), split(g[i, low_rows, :])
            par.append(-(dot3_nt(split(um[p]), root) + dot3_nt(split(lm_t[p]), g_mine)))
            own.append(
                dot3_nt(split(ll_t[i]), split(ll_t[i, low_rows, :])) + dot3_nt(split(g[i]), g_mine)
                - dot3_nt(split(ul[i]), root)
            )
        terms[:, :, pl.ds(128 + 64 * pair, 64), :] = jnp.concatenate(par, axis=1).reshape(4, 4, 64, 128)
        terms[:, :, pl.ds(256 + 32 * pair, 32), :] = jnp.concatenate(own, axis=1).reshape(4, 4, 32, 128)
    half = DIAG_ROWS // 4

    def outs(base):
        return [out.at[pl.ds(base + half * h, half), :] for h in range(2)]

    sc = TorusScatter(
        net,
        lambda o, h: terms.at[o, :, pl.ds(half * h, half), :],
        lambda o, h: terms.at[:, o, pl.ds(2 * half + half * h, half), :],
        bufs_xz, bufs_zx,
    )
    sc.start()
    sc.plain()
    sc.middle()
    sc.turn()
    sc.second_middle()
    sc.end(outs(0), outs(2 * half))
    net.finish()


def third_step(parent, *arrays):
    return pl.pallas_call(
        third_kernel,
        out_shape=jax.ShapeDtypeStruct((DIAG_ROWS, 128), F32),
        in_specs=[pl.BlockSpec(memory_space=pltpu.SMEM)] + [pl.BlockSpec(memory_space=VMEM)] * 7,
        out_specs=pl.BlockSpec(memory_space=VMEM),
        scratch_shapes=[
            VMEM((4, 4, DIAG_ROWS, 128), F32), VMEM((MIDS, MID, 64), F32), VMEM((LOWS, LOW, 32), F32),
        ] + torus_bufs(DIAG_ROWS // 4, 128) + torus_bufs(DIAG_ROWS // 4, 128) + [
            pltpu.SemaphoreType.DMA((32,)),
            pltpu.SemaphoreType.DMA((32,)),
        ],
        compiler_params=params(1),
        name="third_step",
    )(parent, *arrays)


def lower_part(factor):
    rows_here = factor.shape[1]
    row_ids = lax.axis_index("col") * rows_here + lax.broadcasted_iota(jnp.int32, factor.shape[1:], 0)
    col_ids = lax.broadcasted_iota(jnp.int32, factor.shape[1:], 1)
    return jnp.where((col_ids <= row_ids)[None], factor, 0.0)


def live_mask(local_rows, first_row, structure, block_shift):
    row_ids = first_row + jnp.arange(local_rows, dtype=jnp.int32)
    block_ids = row_ids // BLOCK + block_shift
    return jnp.any(block_ids[None, :, None] == structure[:, None, :], axis=2).astype(F32)


def local(root_factor, mid_factor, low_factor, mid_rows, low_parent_rows, low_root_rows, mid_struct, low_struct, low_parent):
    row = lax.axis_index("row")
    lm = lower_part(mid_factor)
    ll = lower_part(low_factor)
    m = jnp.transpose(mid_rows, (0, 2, 1)) * live_mask(512, row * 512, mid_struct, 0)[:, None, :]
    r = jnp.transpose(low_root_rows, (0, 2, 1)) * live_mask(512, row * 512, low_struct, MID // BLOCK)[:, None, :]
    p = jnp.transpose(low_parent_rows, (0, 2, 1)) * live_mask(128, row * 128, low_struct, 0)[:, None, :]
    sigma, mid_cross, low_root, g, um_c, ul_c, _, _ = main_step(low_parent, root_factor, lm, m, r, p, ll)
    sums = third_step(low_parent, mid_cross, low_root, um_c, ul_c, g, lm, ll)
    mid_diag = jnp.transpose(sums[:128].reshape(2, 64, 128), (0, 2, 1))
    par = sums[128:256].reshape(2, 64, 2, 64)
    low_cross_parent = jnp.transpose(par, (0, 2, 3, 1)).reshape(4, 64, 64)
    low = sums[256:].reshape(2, 32, 2, 64)
    low_diag = jnp.transpose(low, (0, 2, 3, 1)).reshape(4, 64, 32)
    return sigma, mid_diag, mid_cross, low_diag, low_cross_parent, low_root


def solution(mesh):
    rc = P(None, "row", "col")
    in_specs = (P("col", None), P(None, "col", None), P(None, "col", None), rc, rc, rc, P(), P(), P())
    out_specs = (P("row", "col"), rc, rc, rc, rc, rc)
    return jax.shard_map(local, mesh=mesh, in_specs=in_specs, out_specs=out_specs, check_vma=False)
```

```python
import functools

import jax
import jax.numpy as jnp
from jax import lax
from jax.experimental import pallas as pl
from jax.experimental.pallas import tpu as pltpu
from jax.sharding import PartitionSpec as P

BLOCK = 256
ROOT = 4096
MID = 1024
LOW = 512
MIDS = 2
LOWS = 4
MESH = pl.DeviceIdType.MESH
F32 = jnp.float32
VMEM = pltpu.VMEM
ANY = pl.ANY


class Net:
    def __init__(self, send_sem, recv_sem):
        self.row = lax.axis_index("row")
        self.col = lax.axis_index("col")
        self.place = {
            "x": lax.div(self.col, 4),
            "z": lax.rem(self.col, 4),
            "y": lax.div(self.row, 2),
            "core": lax.rem(self.row, 2),
        }
        self.send_sem, self.recv_sem, self.used, self.started = send_sem, recv_sem, 0, []

    def at(self, axis, shift):
        if axis == "core":
            return lax.rem(self.place["core"] + shift, 2)
        return lax.rem(self.place[axis] + shift + 4, 4)

    def device(self, **shifts):
        at = {axis: self.at(axis, shifts.get(axis, 0)) for axis in self.place}
        return (at["y"] * 2 + at["core"], at["x"] * 4 + at["z"])

    def greet(self, axes, wait=True):
        barrier = pltpu.get_barrier_semaphore()
        count = 0
        for axis in axes:
            for shift in (1,) if axis == "core" else (1, -1):
                pl.semaphore_signal(barrier, inc=1, device_id=self.device(**{axis: shift}), device_id_type=MESH)
                count += 1
        if wait:
            self.met(count)

    def met(self, count):
        pl.semaphore_wait(pltpu.get_barrier_semaphore(), count)

    def send(self, src, dst, axis, shift):
        index = self.used
        self.used += 1
        copy = pltpu.make_async_remote_copy(
            src_ref=src,
            dst_ref=dst,
            send_sem=self.send_sem.at[index],
            recv_sem=self.recv_sem.at[index],
            device_id=self.device(**{axis: shift}),
            device_id_type=MESH,
        )
        copy.start()
        self.started.append(copy)
        return copy

    def finish(self):
        for copy in self.started:
            copy.wait_send()


def mult(value, unit):
    return pl.multiple_of(value, unit)


def params(collective_id):
    return pltpu.CompilerParams(collective_id=collective_id, has_side_effects=True, vmem_limit_bytes=62 * 2**20)


class Gather:
    def __init__(self, net, src, dst, whole, half, first, second, local_sem, share=None):
        self.net, self.dst, self.whole, self.half = net, dst, whole, half
        self.first, self.second, self.share = first, second, share
        self.src, self.local_sem, self.sent = src, local_sem, []

    def send(self, *args):
        copy = self.net.send(*args)
        self.sent.append(copy)
        return copy

    def free(self):
        for copy in self.sent:
            copy.wait_send()
        self.net.started = [copy for copy in self.net.started if not any(copy is one for one in self.sent)]

    def spot(self, a, b):
        at = {self.first: self.net.at(self.first, a), self.second: self.net.at(self.second, b)}
        return at["x"], at["z"]

    def piece(self, a, b):
        return self.whole(self.dst, *self.spot(a, b))

    def part(self, a, b, h):
        return self.half(self.dst, *self.spot(a, b), h)

    def start(self):
        net, own = self.net, self.piece(0, 0)
        self.local = pltpu.make_async_copy(self.src, own, self.local_sem)
        self.local.start()
        self.p1 = [self.send(self.src, own, self.first, s) for s in (1, -1)]
        self.p2 = {0: [self.send(self.src, own, self.second, s) for s in (1, -1)]}

    def onward(self, a):
        piece = self.piece(a, 0)
        self.p2[a] = [self.send(piece, piece, self.second, s) for s in (1, -1)]

    def first_ring(self):
        self.fwd = []
        for index, shift in enumerate((1, -1)):
            self.p1[index].wait_recv()
            part = self.part(-shift, 0, index)
            self.fwd.append(self.send(part, part, self.first, shift))
            self.onward(-shift)

    def first_end(self):
        for copy in self.fwd:
            copy.wait_recv()
        self.onward(2)

    def second_ring(self, a):
        copies = []
        for index, shift in enumerate((1, -1)):
            self.p2[a][index].wait_recv()
            part = self.part(a, -shift, index)
            copies.append(self.send(part, part, self.second, shift))
        self.p2[a] = copies

    def second_end(self, a):
        for copy in self.p2[a]:
            copy.wait_recv()

    def finish(self):
        self.local.wait()


class Scatter:
    def __init__(self, net, axis, part, near, far):
        self.net, self.axis, self.part, self.near, self.far = net, axis, part, near, far

    def start(self):
        opposite = self.net.at(self.axis, 2)
        self.first = [
            self.net.send(self.part(opposite, h), self.near[h], self.axis, shift) for h, shift in enumerate((1, -1))
        ]

    def plain(self):
        self.second = [
            self.net.send(self.part(self.net.at(self.axis, shift), 1 - h), self.far[h][1 - h], self.axis, shift)
            for h, shift in enumerate((1, -1))
        ]

    def middle(self):
        for h, shift in enumerate((1, -1)):
            self.first[h].wait_recv()
            self.near[h][...] += self.part(self.net.at(self.axis, shift), h)[...]
            self.second.append(self.net.send(self.near[h], self.far[h][h], self.axis, shift))

    def end(self, out):
        for copy in self.second:
            copy.wait_recv()
        for h in range(2):
            out[h][...] = self.part(self.net.at(self.axis, 0), h)[...] + self.far[0][h][...] + self.far[1][h][...]


class TorusScatter:
    def __init__(self, net, part_xz, part_zx, bufs_xz, bufs_zx):
        self.net, self.bufs = net, (bufs_xz, bufs_zx)
        self.stages = [self.stage(axis, part, bufs[0], bufs[1])
                       for axis, part, bufs in (("x", part_xz, bufs_xz), ("z", part_zx, bufs_zx))]

    def stage(self, axis, part, near, far):
        return Scatter(self.net, axis, part, [near.at[0], near.at[1]], [[far.at[s, h] for h in range(2)] for s in range(2)])

    def start(self):
        for stage in self.stages:
            stage.start()

    def plain(self):
        for stage in self.stages:
            stage.plain()

    def middle(self):
        for stage in self.stages:
            stage.middle()

    def turn(self):
        later = []
        for stage, axis, bufs in zip(self.stages, ("z", "x"), self.bufs):
            sums = bufs[2]
            stage.end([sums.at[0], sums.at[1]])
            part = functools.partial(lambda sums, o, h: sums.at[h, o], sums)
            later.append(self.stage(axis, part, bufs[3], bufs[4]))
            later[-1].start()
            later[-1].plain()
        self.stages = later

    second_middle = middle

    def end(self, out_xz, out_zx):
        for stage, out in zip(self.stages, (out_xz, out_zx)):
            stage.end(out)


def torus_bufs(rows, lanes):
    return [
        VMEM((2, 4, rows, lanes), F32),
        VMEM((2, 2, 4, rows, lanes), F32),
        VMEM((2, 4, rows, lanes), F32),
        VMEM((2, rows, lanes), F32),
        VMEM((2, 2, rows, lanes), F32),
    ]


def split(a):
    high = a.astype(jnp.bfloat16)
    return high, (a - high.astype(F32)).astype(jnp.bfloat16)


def dot3(a, b):
    go = functools.partial(jnp.dot, preferred_element_type=F32)
    return go(a[0], b[0]) + (go(a[0], b[1]) + go(a[1], b[0]))


class Ring:
    def __init__(self, net, pieces, halves, share=True):
        self.net, self.pieces, self.halves, self.share = net, pieces, halves, share

    def pair_up(self, place):
        if self.share:
            self.pair += [self.net.send(part, part, "core", 1) for part in self.pieces(place)]

    def start(self):
        own = self.pieces(self.net.at("y", 0))
        self.near = [[self.net.send(part, part, "y", s) for part in own] for s in (1, -1)]
        self.pair = []
        self.pair_up(self.net.at("y", 0))

    def middle(self):
        self.far = []
        for index, shift in enumerate((1, -1)):
            for copy in self.near[index]:
                copy.wait_recv()
            place = self.net.at("y", -shift)
            self.far += [self.net.send(part, part, "y", shift) for part in self.halves(place, index)]
            self.pair_up(place)

    def end(self):
        for copy in self.far:
            copy.wait_recv()
        self.pair_up(self.net.at("y", 2))

    def finish(self):
        for copy in self.pair:
            copy.wait_recv()


CHUNKS = 4
STEP = 256


class Spread:
    def __init__(self, net, source, out, send_sem, recv_sem, local_sem):
        self.net, self.source, self.out = net, source, out
        self.send_sem, self.recv_sem, self.local_sem = send_sem, recv_sem, local_sem
        x, z = net.place["x"], net.place["z"]
        self.lanes = pl.ds(mult(lax.rem(z, 2) * 256, 256), 256)
        self.away = lax.rem(net.place["y"] - x + 4, 4)
        self.is_core = net.place["core"] == lax.div(z, 2)

    def spot(self, ref, way, chunk, lanes):
        per = ref.shape[1] // STEP
        return ref.at[way * (ref.shape[0] // 2) + chunk // per, pl.ds(chunk % per * STEP, STEP), lanes]

    def copy(self, way, chunk, pair):
        place = self.spot(self.out, way, chunk, slice(None))
        index = pair * 2 * CHUNKS + way * CHUNKS + chunk
        to = {"core": 1} if pair else {"y": 1 - 2 * way}
        return pltpu.make_async_remote_copy(
            src_ref=place, dst_ref=place,
            send_sem=self.send_sem.at[index], recv_sem=self.recv_sem.at[index],
            device_id=self.net.device(**to), device_id_type=MESH,
        )

    def load(self):
        return pltpu.make_async_copy(self.source.at[:, :, self.lanes], self.out, self.local_sem)

    def start(self):
        @pl.when(jnp.logical_and(self.is_core, self.away == 0))
        def _():
            self.load().start()
            self.load().wait()
            for pair in range(2):
                for chunk in range(CHUNKS):
                    for way in range(2):
                        self.copy(way, chunk, pair).start()

    def onward(self, first, last):
        for away in (1, 2, 3):
            @pl.when(jnp.logical_and(self.is_core, self.away == away))
            def _():
                for step in range(first, last):
                    for way in range(2):
                        hops = away if way == 0 else 4 - away
                        chunk = step + 1 - hops
                        if 0 <= chunk < CHUNKS:
                            self.copy(way, chunk, 0).wait_recv()
                            if hops < 3:
                                self.copy(way, chunk, 0).start()
                            self.copy(way, chunk, 1).start()

    def finish(self):
        for chunk in range(CHUNKS):
            for way in range(2):
                @pl.when(jnp.logical_and(self.is_core, self.away != (3, 1)[way]))
                def _():
                    self.copy(way, chunk, 0).wait_send()

                @pl.when(self.is_core)
                def _():
                    self.copy(way, chunk, 1).wait_send()

                @pl.when(jnp.logical_not(self.is_core))
                def _():
                    self.copy(way, chunk, 1).wait_recv()


def dot3_nt(a, b):
    go = lambda s, t: lax.dot_general(s, t, (((1,), (1,)), ((), ())), preferred_element_type=F32)
    return go(a[0], b[0]) + (go(a[0], b[1]) + go(a[1], b[0]))


def main_kernel(parent, lr, lm_own, m, r, p, ll, sigma, out_m, out_l, g, um_c, ul_c, lm_all, p_all,
                m_all, r_all, p_mine, g_in, ll_all, stage, high, low, s_high, s_low, terms, cm, cl,
                acc_m, acc_l, core_m, core_l, near_m, near_l, far_m, far_l, *scratch):
    bufs_xz, bufs_zx, (send_sem, recv_sem, spread_send, spread_recv, local_sem, load_sem) = (
        scratch[:5], scratch[5:10], scratch[10:]
    )
    net = Net(send_sem, recv_sem)
    core, y = net.place["core"], net.place["y"]
    other = 1 - core

    def band(block):
        return pl.ds(block * 256, 256)

    def root_block(b):
        return cm.at[b // 4, band(b % 4), :] if b < 8 else cl.at[(b - 8) // 2, band(b % 2), :]

    root_loads = [
        pltpu.make_async_copy(
            lr.at[pl.ds(128 * t, 128), pl.ds(mult(net.row * 512 + 256 * h, 256), 256)], acc_m.at[h, t], load_sem.at[2 * h + t]
        )
        for h in range(2)
        for t in range(2)
    ]
    root_loads += [pltpu.make_async_copy(lr.at[:, band(b)], root_block(b), load_sem.at[4 + b]) for b in range(16)]
    for load in root_loads:
        load.start()
    net.greet(("x", "z", "y", "core"))

    def rows(x, z, n):
        return pl.ds(mult((x * 4 + z) * n, n), n)

    def eighth(n):
        return pl.ds(mult(y * n, n), n)

    two = pl.ds(2 * core, 2)
    def p_lanes(o):
        return pl.ds(mult(o * 256, 256), 256)

    ring_p = Ring(net, lambda o: [p_mine.at[:, :, p_lanes(o)]], lambda o, h: [p_mine.at[h, :, p_lanes(o)]], share=False)
    ga_ps = tuple(
        Gather(
            net, p_mine.at[h], p_all,
            lambda ref, x, z, h=h: ref.at[2 * core + h, rows(x, z, 32), :],
            lambda ref, x, z, part, h=h: ref.at[2 * core + h, pl.ds(mult((x * 4 + z) * 32 + 16 * part, 16), 16), :],
            first, second, local_sem.at[(0, 5)[h]],
        )
        for h, (first, second) in enumerate((("x", "z"), ("z", "x")))
    )
    ga_ll = Gather(
        net, ll.at[two, eighth(8), :], ll_all,
        lambda ref, x, z: ref.at[two, x * 4 + z, eighth(8), :],
        lambda ref, x, z, h: ref.at[2 * core + h, x * 4 + z, eighth(8), :],
        "z", "x", local_sem.at[1],
    )
    ga_lm = Gather(
        net, lm_own.at[core, eighth(16), :], lm_all,
        lambda ref, x, z: ref.at[core, x * 4 + z, eighth(16), :],
        lambda ref, x, z, h: ref.at[core, x * 4 + z, pl.ds(mult(y * 16 + 8 * h, 8), 8), :],
        "x", "z", local_sem.at[2],
    )
    ga_m = Gather(
        net, m, m_all,
        lambda ref, x, z: ref.at[:, rows(x, z, 64), :],
        lambda ref, x, z, h: ref.at[h, rows(x, z, 64), :],
        "x", "z", local_sem.at[3],
    )
    ga_r = Gather(
        net, r, r_all,
        lambda ref, x, z: ref.at[:, rows(x, z, 32), :],
        lambda ref, x, z, h: ref.at[pl.ds(2 * h, 2), rows(x, z, 32), :],
        "z", "x", local_sem.at[4],
    )
    def ll_parts(o):
        return [ll_all.at[two, pl.ds(8 * g, 8), pl.ds(mult(o * 8, 8), 8), pl.ds(0, 256 * (g + 1))] for g in range(2)]

    def lm_parts(o):
        return [
            lm_all.at[core, pl.ds(4 * g, 4), pl.ds(mult(o * 16, 16), 16), pl.ds(0, 256 * (g + 1))] for g in range(4)
        ]

    ring_ll = Ring(net, ll_parts, lambda o, h: ll_parts(o)[1:] if h else ll_parts(o)[:1])
    ring_lm = Ring(net, lm_parts, lambda o, h: lm_parts(o)[:3] if h else lm_parts(o)[3:])

    mine = pl.ds(mult(net.row * 128, 128), 128)
    local_p = pltpu.make_async_copy(p.at[two], p_mine.at[:, :, mine], local_sem.at[5])
    local_p.start()
    pair_p = net.send(p.at[pl.ds(2 * other, 2)], p_mine.at[:, :, mine], "core", 1)
    small, large = (ga_ll, ga_lm), (ga_m, ga_r)
    for item in small + large:
        item.start()
    local_p.wait()
    pair_p.wait_recv()
    ring_p.start()

    base = net.col * 256

    def lower(block, first):
        at = lambda axis: lax.broadcasted_iota(jnp.int32, (256, 256), axis)
        return jnp.where(first + at(1) <= base + at(0), block, 0.0)

    for load in root_loads:
        load.wait()
    for h in range(2):
        block = lower(acc_m[h].reshape(256, 256), net.row * 512 + 256 * h)
        high[0, band(h), :256], low[0, band(h), :256] = split(jnp.transpose(block))
    left = lambda: (high[0, :512, :256], low[0, :512, :256])

    def root_terms(first, last):
        @pl.loop(first, last)
        def _(b):
            block = lower(cm[lax.div(b, 4), pl.ds(mult(lax.rem(b, 4) * 256, 256), 256), :], b * 256)
            terms[lax.div(b, 4), lax.rem(b, 4)] = dot3(left(), split(block))
            block = lower(cl[lax.div(b, 2), pl.ds(mult(lax.rem(b, 2) * 256, 256), 256), :], b * 256 + 2048)
            terms[2 + lax.div(b, 4), lax.rem(b, 4)] = dot3(left(), split(block))

    sc = TorusScatter(
        net,
        lambda o, h: terms.at[o, :, pl.ds(128 * h, 128), :],
        lambda o, h: terms.at[:, o, pl.ds(256 + 128 * h, 128), :],
        bufs_xz, bufs_zx,
    )
    ring_p.middle()
    ring_p.end()
    for item in ga_ps:
        item.start()
    for item in small:
        item.first_ring()
    for item in small:
        item.first_end()
    for item in large:
        item.first_ring()
    for a in (0, -1, 1, 2):
        for item in small:
            item.second_ring(a)
    for item in large:
        item.first_end()
    for item in small:
        for a in (0, -1, 1, 2):
            item.second_end(a)
        item.finish()
    ring_ll.start()
    ring_lm.start()
    for item in ga_ps:
        item.first_ring()
    for item in large:
        item.second_ring(0)
    root_terms(0, 3)
    for item in ga_ps:
        item.first_end()
    ring_ll.middle()
    ring_lm.middle()
    for a in (-1, 1):
        for item in large:
            item.second_ring(a)
    root_terms(3, 5)
    for a in (0, -1, 1):
        for item in ga_ps:
            item.second_ring(a)
    for item in large + ga_ps:
        item.second_ring(2)
    root_terms(5, 8)
    sc.start()
    sc.plain()
    ring_ll.end()
    ring_lm.end()
    ring_lm.finish()
    lm_loads = [pltpu.make_async_copy(lm_all.at[k], stage.at[k], load_sem.at[k]) for k in range(MIDS)]
    for load in lm_loads:
        load.start()
    for item in large:
        for a in (0, -1, 1, 2):
            item.second_end(a)
        item.finish()
    spread_m = Spread(net, m_all, um_c, spread_send.at[0], spread_recv.at[0], local_sem.at[6])
    spread_l = Spread(net, r_all, ul_c, spread_send.at[1], spread_recv.at[1], local_sem.at[7])
    spread_m.start()
    spread_l.start()

    def mid_nodes(lanes):
        for load in lm_loads:
            load.wait()

        @pl.loop(0, MIDS)
        def _(k):
            for j in range(4):
                total = None
                for t in range(j, 4):
                    tile = jnp.transpose(stage[k, pl.ds(4 * t, 4), :, band(j)].reshape(256, 256))
                    term = dot3(split(tile), split(m_all[k, band(t), lanes]))
                    total = term if total is None else total + term
                m_all[k, band(j), lanes] = total
                high[k, band(j), lanes], low[k, band(j), lanes] = split(total)

    ga_m.free()
    mid_nodes(pl.ds(0, 512))
    for item in ga_ps:
        for a in (0, -1, 1, 2):
            item.second_end(a)
        item.finish()
    shared_p = []
    for o in range(4):
        part = p_all.at[two, pl.ds(128 * o, 128), :]
        shared_p.append(net.send(part, part, "core", 1))
    sc.middle()
    ring_ll.finish()
    for copy in shared_p:
        copy.wait_recv()
    p_loads = [
        pltpu.make_async_copy(p_all.at[i, pl.ds(64 * t, 64), :], stage.at[i // 2, i % 2 * 8 + t], load_sem.at[8 * i + t])
        for i in range(LOWS)
        for t in range(8)
    ]
    for load in p_loads:
        load.start()

    def low_nodes(first, lanes, with_g):
        for load in p_loads[8 * first : 8 * first + 16]:
            load.wait()

        @pl.loop(first, first + 2)
        def _(i):
            k = parent[i]
            own = split(lm_own[k]) if with_g else None
            for t in range(2):
                p_both = split(stage[first // 2, pl.ds((i - first) * 8 + 4 * t, 4), :, :].reshape(256, MID))
                r_all[i, band(t), lanes] -= dot3(p_both, (high[k, :, lanes], low[k, :, lanes]))
                if with_g:
                    g_in[band(t), :] = dot3_nt(p_both, own)
            for j in range(2):
                total, g_total = None, None
                for t in range(j, 2):
                    tile = split(jnp.transpose(ll_all[i, pl.ds(8 * t, 8), :, band(j)].reshape(256, 256)))
                    term = dot3(tile, split(r_all[i, band(t), lanes]))
                    total = term if total is None else total + term
                    if with_g:
                        term = dot3(tile, split(g_in[band(t), :]))
                        g_total = term if g_total is None else g_total + term
                r_all[i, band(j), lanes] = total
                if with_g:
                    g[i, band(j), :] = g_total

    both_onward = lambda first, last: (spread_m.onward(first, last), spread_l.onward(first, last))
    ga_r.free()
    both_onward(0, 1)
    low_nodes(0, pl.ds(0, 512), True)
    sc.turn()
    both_onward(1, 3)
    sc.second_middle()
    low_nodes(2, pl.ds(0, 512), True)
    both_onward(3, 5)
    for load in lm_loads:
        load.start()
    outs = lambda first: [sigma.at[pl.ds(first + 128 * h, 128), :] for h in range(2)]
    sc.end(outs(0), outs(256))
    s_high[...], s_low[...] = split(sigma[...])

    def slab(ref, unit, d, k):
        return ref.at[:, pl.ds(mult((2 * net.at("y", d) + k) * unit, unit), unit), :]

    def multiply(d, k):
        both = (slab(high, 128, d, k)[...].reshape(256, 512), slab(low, 128, d, k)[...].reshape(256, 512))
        slab(cm, 128, d, k)[...] = -dot3(both, (s_high[...], s_low[...])).reshape(MIDS, 128, 256)
        both = split(slab(r_all, 64, d, k)[...].reshape(256, 512))
        slab(cl, 64, d, k)[...] = -dot3(both, (s_high[...], s_low[...])).reshape(LOWS, 64, 256)

    order = (2, 1, -1, 0)
    pairs = {}
    for d in order:
        multiply(d, other)
        pairs[d] = [
            net.send(slab(cm, 128, d, other), core_m.at[d % 4], "core", 1),
            net.send(slab(cl, 64, d, other), core_l.at[d % 4], "core", 1),
        ]
    firsts = []
    for d in order:
        if d == -1:
            both_onward(5, CHUNKS + 2)
        multiply(d, core)
        for copy in pairs[d]:
            copy.wait_recv()
        acc_m[d % 4] = core_m[d % 4] + slab(cm, 128, d, core)[...]
        acc_l[d % 4] = core_l[d % 4] + slab(cl, 64, d, core)[...]
        if d == 2:
            firsts = [net.send(acc_m.at[2], near_m, "y", 1), net.send(acc_l.at[2], near_l, "y", -1)]
    seconds = [net.send(acc_l.at[1], far_l.at[0], "y", 1), net.send(acc_m.at[3], far_m.at[1], "y", -1)]

    block_column = pl.ds(0, 256)
    spread_m.finish()
    spread_l.finish()
    column_loads = [
        pltpu.make_async_copy(src, dst.at[:, :, block_column], local_sem.at[index])
        for index, (src, dst) in enumerate(((um_c, m_all), (ul_c, r_all)))
    ]
    for load in column_loads:
        load.start()
    for load in column_loads:
        load.wait()
    mid_nodes(block_column)
    for load in p_loads:
        load.start()
    column_out = [
        pltpu.make_async_copy(src.at[:, :, block_column], dst, local_sem.at[index])
        for index, (dst, src) in enumerate(((um_c, m_all), (ul_c, r_all)))
    ]
    column_out[0].start()
    firsts[0].wait_recv()
    near_m[...] += acc_m[1]
    seconds.append(net.send(near_m, far_m.at[0], "y", 1))
    firsts[1].wait_recv()
    near_l[...] += acc_l[3]
    seconds.append(net.send(near_l, far_l.at[1], "y", -1))
    low_nodes(0, block_column, False)
    low_nodes(2, block_column, False)
    column_out[1].start()
    for copy in seconds:
        copy.wait_recv()
    out_m[...] = acc_m[0] + far_m[0] + far_m[1]
    out_l[...] = acc_l[0] + far_l[0] + far_l[1]
    for copy in column_out:
        copy.wait()
    net.finish()


SEMS = 240


def main_step(*arrays):
    shape = lambda *dims: jax.ShapeDtypeStruct(dims, F32)
    vmem, hbm = pl.BlockSpec(memory_space=VMEM), pl.BlockSpec(memory_space=ANY)
    block = lambda *dims: VMEM(dims, F32)
    half = lambda *dims: VMEM(dims, jnp.bfloat16)
    return pl.pallas_call(
        main_kernel,
        out_shape=(
            shape(512, 256), shape(MIDS, 128, 256), shape(LOWS, 64, 256), shape(LOWS, LOW, 64),
            shape(MIDS, MID, 256), shape(LOWS, LOW, 256), shape(MIDS, 16, 64, MID), shape(LOWS, LOW, MID),
        ),
        in_specs=[pl.BlockSpec(memory_space=pltpu.SMEM), hbm, vmem] + [hbm] * 4,
        out_specs=[vmem] * 4 + [hbm] * 4,
        scratch_shapes=[
            block(MIDS, MID, 512), block(LOWS, LOW, 512), block(2, 32, MID), block(LOW, 64),
            block(LOWS, 16, 32, LOW), block(MIDS, 16, 64, MID), half(MIDS, MID, 512), half(MIDS, MID, 512),
            half(512, 256), half(512, 256), block(4, 4, 512, 256), block(MIDS, MID, 256), block(LOWS, LOW, 256),
            block(4, MIDS, 128, 256), block(4, LOWS, 64, 256), block(4, MIDS, 128, 256), block(4, LOWS, 64, 256),
            block(MIDS, 128, 256), block(LOWS, 64, 256), block(2, MIDS, 128, 256), block(2, LOWS, 64, 256),
        ] + torus_bufs(128, 256) + torus_bufs(128, 256) + [
            pltpu.SemaphoreType.DMA((SEMS,)),
            pltpu.SemaphoreType.DMA((SEMS,)),
            pltpu.SemaphoreType.DMA((2, 4 * CHUNKS)),
            pltpu.SemaphoreType.DMA((2, 4 * CHUNKS)),
            pltpu.SemaphoreType.DMA((8,)),
            pltpu.SemaphoreType.DMA((32,)),
        ],
        compiler_params=params(0),
        name="main_step",
    )(*arrays)


DIAG_ROWS = 320


def third_kernel(parent, mid_cross, low_root, um, ul, g, lm, ll, out, terms, lm_t, ll_t, *scratch):
    bufs_xz, bufs_zx, (send_sem, recv_sem) = scratch[:5], scratch[5:10], scratch[10:]
    net = Net(send_sem, recv_sem)
    net.greet(("x", "z"), wait=False)
    for p in range(MIDS):
        lm_t[p] = jnp.transpose(lm[p])
    for i in range(LOWS):
        ll_t[i] = jnp.transpose(ll[i])
    low_rows = pl.ds(mult(net.row * 64, 64), 64)
    for p in range(MIDS):
        mine = split(lm_t[p, pl.ds(mult(net.row * 128, 128), 128), :])
        term = dot3_nt(split(lm_t[p]), mine) - dot3_nt(split(um[p]), split(mid_cross[p]))
        terms[:, :, pl.ds(64 * p, 64), :] = term.reshape(4, 4, 64, 128)
    for pair in range(2):
        par, own = [], []
        for i in (2 * pair, 2 * pair + 1):
            p = parent[i]
            root, g_mine = split(low_root[i]), split(g[i, low_rows, :])
            par.append(-(dot3_nt(split(um[p]), root) + dot3_nt(split(lm_t[p]), g_mine)))
            own.append(
                dot3_nt(split(ll_t[i]), split(ll_t[i, low_rows, :])) + dot3_nt(split(g[i]), g_mine)
                - dot3_nt(split(ul[i]), root)
            )
        terms[:, :, pl.ds(128 + 64 * pair, 64), :] = jnp.concatenate(par, axis=1).reshape(4, 4, 64, 128)
        terms[:, :, pl.ds(256 + 32 * pair, 32), :] = jnp.concatenate(own, axis=1).reshape(4, 4, 32, 128)
    half = DIAG_ROWS // 4

    def outs(base):
        return [out.at[pl.ds(base + half * h, half), :] for h in range(2)]

    sc = TorusScatter(
        net,
        lambda o, h: terms.at[o, :, pl.ds(half * h, half), :],
        lambda o, h: terms.at[:, o, pl.ds(2 * half + half * h, half), :],
        bufs_xz, bufs_zx,
    )
    net.met(4)
    sc.start()
    sc.plain()
    sc.middle()
    sc.turn()
    sc.second_middle()
    sc.end(outs(0), outs(2 * half))
    net.finish()


def third_step(parent, *arrays):
    return pl.pallas_call(
        third_kernel,
        out_shape=jax.ShapeDtypeStruct((DIAG_ROWS, 128), F32),
        in_specs=[pl.BlockSpec(memory_space=pltpu.SMEM)] + [pl.BlockSpec(memory_space=VMEM)] * 7,
        out_specs=pl.BlockSpec(memory_space=VMEM),
        scratch_shapes=[
            VMEM((4, 4, DIAG_ROWS, 128), F32), VMEM((MIDS, MID, 64), F32), VMEM((LOWS, LOW, 32), F32),
        ] + torus_bufs(DIAG_ROWS // 4, 128) + torus_bufs(DIAG_ROWS // 4, 128) + [
            pltpu.SemaphoreType.DMA((32,)),
            pltpu.SemaphoreType.DMA((32,)),
        ],
        compiler_params=params(1),
        name="third_step",
    )(parent, *arrays)


def lower_part(factor):
    rows_here = factor.shape[1]
    row_ids = lax.axis_index("col") * rows_here + lax.broadcasted_iota(jnp.int32, factor.shape[1:], 0)
    col_ids = lax.broadcasted_iota(jnp.int32, factor.shape[1:], 1)
    return jnp.where((col_ids <= row_ids)[None], factor, 0.0)


def live_mask(local_rows, first_row, structure, block_shift):
    row_ids = first_row + jnp.arange(local_rows, dtype=jnp.int32)
    block_ids = row_ids // BLOCK + block_shift
    return jnp.any(block_ids[None, :, None] == structure[:, None, :], axis=2).astype(F32)


def local(root_factor, mid_factor, low_factor, mid_rows, low_parent_rows, low_root_rows, mid_struct, low_struct, low_parent):
    row = lax.axis_index("row")
    lm = lower_part(mid_factor)
    ll = lower_part(low_factor)
    m = jnp.transpose(mid_rows, (0, 2, 1)) * live_mask(512, row * 512, mid_struct, 0)[:, None, :]
    r = jnp.transpose(low_root_rows, (0, 2, 1)) * live_mask(512, row * 512, low_struct, MID // BLOCK)[:, None, :]
    p = jnp.transpose(low_parent_rows, (0, 2, 1)) * live_mask(128, row * 128, low_struct, 0)[:, None, :]
    sigma, mid_cross, low_root, g, um_c, ul_c, _, _ = main_step(low_parent, root_factor, lm, m, r, p, ll)
    sums = third_step(low_parent, mid_cross, low_root, um_c, ul_c, g, lm, ll)
    mid_diag = jnp.transpose(sums[:128].reshape(2, 64, 128), (0, 2, 1))
    par = sums[128:256].reshape(2, 64, 2, 64)
    low_cross_parent = jnp.transpose(par, (0, 2, 3, 1)).reshape(4, 64, 64)
    low = sums[256:].reshape(2, 32, 2, 64)
    low_diag = jnp.transpose(low, (0, 2, 3, 1)).reshape(4, 64, 32)
    return sigma, mid_diag, mid_cross, low_diag, low_cross_parent, low_root


def solution(mesh):
    rc = P(None, "row", "col")
    in_specs = (P("col", None), P(None, "col", None), P(None, "col", None), rc, rc, rc, P(), P(), P())
    out_specs = (P("row", "col"), rc, rc, rc, rc, rc)
    return jax.shard_map(local, mesh=mesh, in_specs=in_specs, out_specs=out_specs, check_vma=False)
```
